512 devices in a mesh: seq: 64 (over y, z), mp: 8 (over x, core).
Axes of the slice: x: 4, y: 8, z: 8, core: 2. Of those that a mesh axis runs over, the one named last changes fastest.
Arguments:
- hidden: bfloat16 [8192, 4096], P('seq', 'mp'), may hold values from -24 to 24
- keys: bfloat16 [8192, 1024], P('seq', 'mp'), may hold values from -3000 to 3000
- values: bfloat16 [8192, 1024], P('seq', 'mp'), may hold values from -24 to 24
- norm_gain: float32 [4096], P('mp'), may hold values from 0.1 to 1.9
- w_query: bfloat16 [4096, 2048], P('mp'), may hold values from -0.09375 to 0.09375
- w_out: bfloat16 [2048, 4096], P(None, 'mp'), may hold values from -0.25 to 0.25
- depth: int32 [64], P('seq'), may hold values from 1 to 3
- cotangent: bfloat16 [8192, 4096], P('seq', 'mp'), may hold values from -6 to 6
Outputs:
- mixed: bfloat16 [8192, 4096], P('seq', 'mp')
- grad_hidden: bfloat16 [8192, 4096], P('seq', 'mp')
The draws below stay inside these ranges and needn't reach their ends.
All inputs are finite; a program needn't handle non-finite values.
Results may differ from the reference program's by a relative error of at most 0.04.
Values may be sent and summed in bfloat16 or wider, within the bound.
A program may use at most 64 MiB of HBM per device.

```python
import jax
import jax.numpy as jnp
from jax import lax

D = 4096
HQ = 16
KVH = 8
HD = 128
BLOCK = 128
TOKENS = 8192
N_MP = 8


def rising_columns(width, low, high):
    column = jnp.arange(width, dtype=jnp.float32)
    return low * jnp.exp(jnp.log(high / low) * column / (width - 1))


def draw_hidden(key, part):
    key = jax.random.fold_in(key, 12)
    noise = jnp.clip(jax.random.normal(key, (TOKENS, D), jnp.float32), -6.0, 6.0)
    column_scale = rising_columns(D, 0.5, 4.0)
    return jnp.clip(noise * column_scale[None, :], -24.0, 24.0).astype(jnp.bfloat16)


def draw_keys(key, part):
    key = jax.random.fold_in(key, 11)
    rows = TOKENS
    width = KVH * HD
    base = 2.0 * jax.random.normal(key, (rows, width), jnp.float32)
    return jnp.clip(base, -3000.0, 3000.0).astype(jnp.bfloat16)


def plant(drawn, key, least, largest):
    index_at = [jax.random.randint(jax.random.fold_in(key, axis), (), 0, length) for axis, length in enumerate(drawn.shape)]
    main_axis = drawn.shape.index(max(drawn.shape))
    beside = index_at[:main_axis] + [(index_at[main_axis] + 1) % drawn.shape[main_axis]] + index_at[main_axis + 1:]
    return drawn.at[tuple(index_at)].set(least).at[tuple(beside)].set(largest)


def levels(own_key, shape, split, smallest, top_value):
    loudness, own = 1.0, jax.random.fold_in(own_key, 6)
    for dim, blocks in split:
        steps = jnp.exp(jax.random.uniform(jax.random.fold_in(own, dim), (blocks,), jnp.float32, smallest / len(split), top_value / len(split)))
        loudness = loudness * jnp.repeat(steps, shape[dim] // blocks).reshape([-1 if axis == dim else 1 for axis in range(len(shape))])
    return loudness


def normal_values(own_key, shape, scale, reach, split=(), kind=jnp.bfloat16):
    entries = scale * jax.random.normal(own_key, shape, jnp.float32)
    if split:
        entries = entries * levels(own_key, shape, split, -0.22, 0.18)
    return jnp.clip(entries, -reach, reach).astype(kind)


def setup_inputs(seed: int = 0) -> dict:
    key_of = jax.random.split(jax.random.key(seed), 9)
    return {
        "hidden": draw_hidden(jax.random.fold_in(key_of[8], 71), 0),
        "keys": draw_keys(jax.random.fold_in(key_of[8], 71), 0),
        "values": normal_values(key_of[2], (TOKENS, KVH * HD), 4.0, 24.0, ((0, 64), (1, 8))),
        "norm_gain": jnp.clip(1.0 + 0.18 * jax.random.normal(key_of[3], (D,), jnp.float32), 0.1, 1.9),
        "w_query": normal_values(key_of[4], (D, HQ * HD), D ** -0.5, 0.09375, ((0, 8),)),
        "w_out": normal_values(key_of[5], (HQ * HD, D), (HQ * HD // 4) ** -0.5, 0.25, ((1, 8),)),
        "depth": plant(jax.random.randint(key_of[6], (TOKENS // BLOCK,), 1, 4), jax.random.fold_in(key_of[6], 1), 1, 3).astype(jnp.int32),
        "cotangent": normal_values(key_of[7], (TOKENS, D), 1.0, 6.0, ((0, 64), (1, 8))),
    }


epsilon = 1e-05
very_low = -1e+30

def reference(hidden, keys, values, norm_gain, w_query, w_out, depth, cotangent):
    length = hidden.shape[0]
    groups = HQ // KVH
    block = min(512, length)
    count = length // block
    scale = HD ** (-0.5)
    part = D // N_MP
    live_depth = jnp.repeat(depth, BLOCK)

    def arrange(rows):
        n_rows = rows.shape[0]
        shaped = rows.reshape(n_rows, KVH, groups, HD)
        return jnp.transpose(shaped, (1, 2, 0, 3)).reshape(KVH, groups * n_rows, HD)

    def restore(grouped, n_rows):
        shaped = grouped.reshape(KVH, groups, n_rows, HD)
        return jnp.transpose(shaped, (2, 0, 1, 3)).reshape(n_rows, HQ * HD)

    def key_block(kidx):
        kstart = kidx * block
        key_part = lax.dynamic_slice_in_dim(keys, kstart, block, 0).reshape(block, KVH, HD).astype(jnp.float32)
        value_part = lax.dynamic_slice_in_dim(values, kstart, block, 0).reshape(block, KVH, HD).astype(jnp.float32)
        key_pos = kstart + jnp.arange(block, dtype=jnp.int32)
        return (key_part, value_part, key_pos)

    def forward_block(index, query, live):
        start = index * block
        grouped = arrange(lax.dynamic_slice_in_dim(query, start, block, 0)).astype(jnp.float32)
        query_pos = jnp.tile(start + jnp.arange(block, dtype=jnp.int32), groups)

        def turn(kidx, state):
            best, total, accum = state
            key_part, value_part, key_pos = key_block(kidx)
            scores = jnp.einsum('kqd,nkd->kqn', grouped, key_part) * scale
            allowed = key_pos[None, :] <= query_pos[:, None]
            block_best = lax.optimization_barrier(jnp.max(jnp.where(allowed, scores, very_low), axis=2))
            weights = jnp.where(allowed, jnp.exp(scores - block_best[:, :, None]), 0.0)
            block_total = lax.optimization_barrier(jnp.sum(weights, axis=2))
            rounded = lax.optimization_barrier(weights.astype(jnp.bfloat16)).astype(jnp.float32)
            block_accum = jnp.einsum('kqn,nkd->kqd', rounded, value_part)
            merged = jnp.maximum(best, block_best)
            old_scale = jnp.exp(best - merged)
            new_scale = jnp.exp(block_best - merged)
            return (merged, total * old_scale + block_total * new_scale, accum * old_scale[:, :, None] + block_accum * new_scale[:, :, None])

        def compute(unused):
            init = (jnp.full((KVH, groups * block), very_low, jnp.float32), jnp.zeros((KVH, groups * block), jnp.float32), jnp.zeros((KVH, groups * block, HD), jnp.float32))
            best, total, accum = lax.fori_loop(0, index + 1, turn, init)
            attended = (accum / total[:, :, None]).astype(jnp.bfloat16)
            return (restore(attended, block), best + jnp.log(total))

        def skip(unused):
            return (jnp.zeros((block, HQ * HD), jnp.bfloat16), jnp.zeros((KVH, groups * block), jnp.float32))
        live_block = jnp.any(lax.dynamic_slice_in_dim(live, start, block, 0))
        return lax.cond(live_block, compute, skip, 0)

    def backward_block(index, query, grad_att, attended, logsum, live):
        start = index * block
        grouped = arrange(lax.dynamic_slice_in_dim(query, start, block, 0)).astype(jnp.float32)
        grad_grouped = arrange(lax.dynamic_slice_in_dim(grad_att, start, block, 0)).astype(jnp.float32)
        out_grouped = arrange(lax.dynamic_slice_in_dim(attended, start, block, 0)).astype(jnp.float32)
        query_pos = jnp.tile(start + jnp.arange(block, dtype=jnp.int32), groups)
        live_rows = jnp.tile(lax.dynamic_slice_in_dim(live, start, block, 0), groups)
        row_logsum = logsum[index]
        deltas = lax.optimization_barrier(jnp.sum(grad_grouped * out_grouped, axis=2))

        def turn(kidx, accum):
            key_part, value_part, key_pos = key_block(kidx)
            scores = jnp.einsum('kqd,nkd->kqn', grouped, key_part) * scale
            allowed = (key_pos[None, :] <= query_pos[:, None]) & live_rows[:, None]
            probs = jnp.where(allowed, jnp.exp(scores - row_logsum[:, :, None]), 0.0)
            dprobs = jnp.einsum('kqd,nkd->kqn', grad_grouped, value_part)
            dscores = lax.optimization_barrier((probs * (dprobs - deltas[:, :, None])).astype(jnp.bfloat16)).astype(jnp.float32)
            return accum + jnp.einsum('kqn,nkd->kqd', dscores, key_part)

        def compute(unused):
            dq = lax.fori_loop(0, index + 1, turn, jnp.zeros((KVH, groups * block, HD), jnp.float32))
            return restore((dq * scale).astype(jnp.bfloat16), block)

        def skip(unused):
            return jnp.zeros((block, HQ * HD), jnp.bfloat16)
        live_block = jnp.any(lax.dynamic_slice_in_dim(live, start, block, 0))
        return lax.cond(live_block, compute, skip, 0)
    indices = jnp.arange(count, dtype=jnp.int32)
    state = hidden
    saved = []
    for level in (2, 3):
        live = live_depth >= level
        live_float = live.astype(jnp.float32)
        state_f = state.astype(jnp.float32)
        inverse = lax.rsqrt(lax.optimization_barrier(jnp.sum(state_f * state_f, axis=1)) / D + epsilon)
        normed = (state_f * inverse[:, None] * norm_gain[None, :]).astype(jnp.bfloat16)
        query = jnp.zeros((length, HQ * HD), jnp.float32)
        for index in range(N_MP):
            partial_value = jnp.dot(normed[:, index * part:(index + 1) * part], w_query[index * part:(index + 1) * part, :], preferred_element_type=jnp.float32)
            query = query + lax.optimization_barrier(partial_value.astype(jnp.bfloat16)).astype(jnp.float32)
        query = query.astype(jnp.bfloat16)
        rows, logsum = lax.map(lambda idx: forward_block(idx, query, live), indices)
        attended = rows.reshape(length, HQ * HD)
        mixed_rows = jnp.dot(attended, w_out, preferred_element_type=jnp.float32)
        saved.append((state, inverse, query, attended, logsum, live, live_float))
        state = (state_f + live_float[:, None] * mixed_rows).astype(jnp.bfloat16)
    grad = cotangent
    for entry in reversed(saved):
        state_in, inverse, query, attended, logsum, live, live_float = entry
        grad_f = grad.astype(jnp.float32)
        grad_mix = (grad_f * live_float[:, None]).astype(jnp.bfloat16)
        grad_att = jnp.zeros((length, HQ * HD), jnp.float32)
        for index in range(N_MP):
            partial_value = jnp.dot(grad_mix[:, index * part:(index + 1) * part], w_out[:, index * part:(index + 1) * part].T, preferred_element_type=jnp.float32)
            grad_att = grad_att + lax.optimization_barrier(partial_value.astype(jnp.bfloat16)).astype(jnp.float32)
        grad_att = grad_att.astype(jnp.bfloat16)
        dq_rows = lax.map(lambda idx: backward_block(idx, query, grad_att, attended, logsum, live), indices)
        grad_query = dq_rows.reshape(length, HQ * HD)
        grad_normed = jnp.dot(grad_query, w_query.T, preferred_element_type=jnp.float32)
        scaled = grad_normed * norm_gain[None, :]
        state_f = state_in.astype(jnp.float32)
        inner = lax.optimization_barrier(jnp.sum(scaled * state_f, axis=1))
        grad_x = inverse[:, None] * scaled - state_f * (inverse ** 3 * inner / D)[:, None]
        grad = (grad_f + grad_x).astype(jnp.bfloat16)
    return (state, grad)
```

```python
import jax
import jax.numpy as jnp
from jax import lax
from jax.experimental import pallas as pl
from jax.experimental.pallas import tpu as pltpu
from jax.sharding import PartitionSpec as P

D = 4096
HD = 128
N_MP = 8
N_Y = 8
N_Z = 8
TOK = 128
ROWS = 2 * TOK
PART = D // N_MP
HEADS = 2048
TILE = HEADS // (N_Y * N_Z)
CHUNK = N_Z * TOK
epsilon = 1e-05
very_low = -1e30
LOG2E = 1.4426950408889634
SCALE = HD ** (-0.5)

MESH = pl.DeviceIdType.MESH
f32 = jnp.float32
bf16 = jnp.bfloat16
ORDER = (4, 3, 5, 2, 6, 1, 7)
NEAR = (1, 7, 2, 6, 3, 5, 4)


def dot_t(a, b):
    return lax.dot_general(a, b, (((1,), (1,)), ((), ())), preferred_element_type=f32)


def dot(a, b):
    return jnp.dot(a, b, preferred_element_type=f32)


def lane_fold(a):
    out = a[:, :128]
    for i in range(1, a.shape[1] // 128):
        out = out + a[:, i * 128 : (i + 1) * 128]
    return out


def lane_max(a):
    out = a[:, :128]
    for i in range(1, a.shape[1] // 128):
        out = jnp.maximum(out, a[:, i * 128 : (i + 1) * 128])
    return out


def row_stat(a):
    return jnp.broadcast_to(jnp.sum(lane_fold(a).T, axis=0, keepdims=True), (8, TOK))


def spread(row):
    return jnp.broadcast_to(row[0:1, :], (TOK, TOK)).T


def widen(a, times):
    return jnp.concatenate([a] * times, axis=1)


def side(a):
    return jnp.concatenate([a[:TOK], a[TOK:]], axis=1)


def stack(a):
    return jnp.concatenate([a[:, :HD], a[:, HD:]], axis=0)


def ring_units(parts, sense):
    whole = [(step, part) for step in (1, 2, 3) for part in range(parts)]
    half = range(parts // 2) if sense > 0 else range(parts // 2, parts)
    return whole + [(4, part) for part in half]


def kernel(
    x_hbm, k_hbm, v_hbm, gain_hbm, wq_hbm, wo_hbm, depth_ref, cot_hbm,
    mixed_ref, grad_ref,
    x_ref, gain_ref, wq_ref, wo_ref, cot_ref,
    kbuf, vbuf, sbuf, pbuf, best_ref,
    part_buf, part_recv, stat_buf, stat_recv,
    rows_buf, rows_recv,
    turned, tile_buf, tile_recv, mf_buf, mb_buf,
    state3,
    load_sem, first_send, first_recv,
    ring_send, ring_recv, tile_ring_send, tile_ring_recv,
    part_send_sem, part_recv_sem, stat_send_sem, stat_recv_sem, rows_send_sem, rows_recv_sem,
    tile_send_sem, tile_recv_sem,
):
    seq = lax.axis_index("seq")
    me = lax.axis_index("mp")
    y = seq // N_Z
    z = seq % N_Z
    pending = []

    def at(yy, zz, mm):
        return (yy * N_Z + zz, mm)

    loads = [
        pltpu.make_async_copy(k_hbm, kbuf.at[y, z], load_sem.at[0]),
        pltpu.make_async_copy(v_hbm, vbuf.at[y, z], load_sem.at[1]),
        pltpu.make_async_copy(x_hbm, x_ref, load_sem.at[2]),
        pltpu.make_async_copy(gain_hbm, gain_ref, load_sem.at[3]),
        pltpu.make_async_copy(wq_hbm, wq_ref, load_sem.at[4]),
        pltpu.make_async_copy(cot_hbm, cot_ref, load_sem.at[5]),
        pltpu.make_async_copy(wo_hbm, wo_ref, load_sem.at[6]),
    ]
    for load in loads:
        load.start()

    barrier = pltpu.get_barrier_semaphore()
    for k in range(1, 8):
        for target in (at(y, z, (me + k) % N_MP), at(y, (z + k) % N_Z, me), at((y + k) % N_Y, z, me)):
            pl.semaphore_signal(barrier, inc=1, device_id=target, device_id_type=MESH)
    pl.semaphore_wait(barrier, 21)

    def send(src, dst, send_sem, recv_sem, target):
        copy = pltpu.make_async_remote_copy(
            src_ref=src, dst_ref=dst, send_sem=send_sem, recv_sem=recv_sem,
            device_id=target, device_id_type=MESH,
        )
        copy.start()
        pending.append(copy)

    def arrived(dst, send_sem, recv_sem, source):
        pltpu.make_async_remote_copy(
            src_ref=dst, dst_ref=dst, send_sem=send_sem, recv_sem=recv_sem,
            device_id=source, device_id_type=MESH,
        ).wait_recv()

    def first_start(which, y_src, z_src, y_buf, z_buf):
        for k in NEAR:
            send(
                y_src, y_buf.at[y, z], first_send.at[which, 0, k], first_recv.at[which, 0, z],
                at(y, (z + k) % N_Z, me),
            )
            send(
                z_src, z_buf.at[y, z], first_send.at[which, 1, k], first_recv.at[which, 1, y],
                at((y + k) % N_Y, z, me),
            )

    def first_wait_y(which, buf, other):
        arrived(buf.at[y, other], first_send.at[which, 0, 0], first_recv.at[which, 0, other], at(y, other, me))

    def first_wait_z(which, buf, other):
        arrived(buf.at[other, z], first_send.at[which, 1, 0], first_recv.at[which, 1, other], at(other, z, me))

    targets = (at((y + 1) % N_Y, z, me), at((y + 7) % N_Y, z, me), at(y, (z + 1) % N_Z, me), at(y, (z + 7) % N_Z, me))
    sources = (targets[1], targets[0], targets[3], targets[2])

    def piece(bufs, parts, stream, unit, shift):
        sense = 1 if stream % 2 == 0 else -1
        step, part = unit
        width = 8 // parts
        turn = {4: (0, 1, 3, 2), 2: (0, 1)}[parts][part]
        if stream < 2:
            start = ((z // width + turn) % parts) * width
            return bufs[0].at[(y + 8 - sense * (step - shift)) % N_Y, pl.ds(start, width)]
        start = ((y // width + turn) % parts) * width
        return bufs[1].at[pl.ds(start, width), (z + 8 - sense * (step - shift)) % N_Z]

    def ring_start(bufs, parts, sems, stream, unit):
        index = ring_units(parts, 1 if stream % 2 == 0 else -1).index(unit)
        ref = piece(bufs, parts, stream, unit, 1)
        send(ref, ref, sems[0].at[stream, index], sems[1].at[stream, index], targets[stream])

    def ring_turn(bufs, parts, sems, index):
        for stream in range(4):
            units = ring_units(parts, 1 if stream % 2 == 0 else -1)
            step, part = units[index]
            ref = piece(bufs, parts, stream, (step, part), 0)
            arrived(ref, sems[0].at[stream, index], sems[1].at[stream, index], sources[stream])
            if (step + 1, part) in units:
                ring_start(bufs, parts, sems, stream, (step + 1, part))

    kv = (kbuf, vbuf)
    kv_sems = (ring_send, ring_recv)
    tiles = (mf_buf, mb_buf)
    tile_sems = (tile_ring_send, tile_ring_recv)

    def kv_inject(part):
        turn = (0, 1, 3, 2)[part]
        if part == 0:
            loads[0].wait()
            loads[1].wait()
            first_wait_y(0, kbuf, z + 1 - 2 * (z % 2))
            first_wait_z(0, vbuf, y + 1 - 2 * (y % 2))
        else:
            for i in range(2):
                first_wait_y(0, kbuf, ((z // 2 + turn) % 4) * 2 + i)
                first_wait_z(0, vbuf, ((y // 2 + turn) % 4) * 2 + i)
        for stream in range(4):
            ring_start(kv, 4, kv_sems, stream, (1, part))

    def part_send(which, peer, k):
        send(
            part_buf.at[which, pl.ds(pl.multiple_of(peer * ROWS, ROWS), ROWS)],
            part_recv.at[which, me],
            part_send_sem.at[which, k], part_recv_sem.at[which, me], at(y, z, peer),
        )

    def part_sum(which):
        total = part_buf[which, pl.ds(pl.multiple_of(me * ROWS, ROWS), ROWS)].astype(f32)
        for k in ORDER:
            peer = (me + k) % N_MP
            arrived(part_recv.at[which, peer], part_send_sem.at[which, 0], part_recv_sem.at[which, peer], at(y, z, peer))
            total = total + part_recv[which, peer].astype(f32)
        return total

    def stat_start(which, row):
        stat_buf[which] = row
        for k in ORDER:
            peer = (me + k) % N_MP
            send(
                stat_buf.at[which], stat_recv.at[which, me],
                stat_send_sem.at[which, k], stat_recv_sem.at[which, me], at(y, z, peer),
            )

    def stat_sum(which):
        total = stat_buf[which]
        for k in ORDER:
            peer = (me + k) % N_MP
            arrived(stat_recv.at[which, peer], stat_send_sem.at[which, 0], stat_recv_sem.at[which, peer], at(y, z, peer))
            total = total + stat_recv[which, peer]
        return total

    def rows_start(which, rows):
        rows_buf[which] = rows
        rows_recv[which, me] = rows
        for k in ORDER:
            peer = (me + k) % N_MP
            send(
                rows_buf.at[which], rows_recv.at[which, me],
                rows_send_sem.at[which, k], rows_recv_sem.at[which, me], at(y, z, peer),
            )

    def rows_wait(which):
        for k in NEAR:
            peer = (me + k) % N_MP
            arrived(rows_recv.at[which, peer], rows_send_sem.at[which, 0], rows_recv_sem.at[which, peer], at(y, z, peer))

    def project(which, product):
        for k in ORDER + (0,):
            peer = (me + k) % N_MP
            cols = product(pl.ds(pl.multiple_of(peer * 256, 256), 256)).astype(bf16)
            part_buf[which, pl.ds(pl.multiple_of(peer * ROWS, ROWS), ROWS)] = stack(cols)
            if k:
                part_send(which, peer, k)

    def project_query(which, state_f):
        scaled = (state_f * gain_ref[...]).astype(bf16)
        project(which, lambda cols: dot(scaled, wq_ref[:, cols]))

    def project_grad(which, rows):
        project(which, lambda cols: dot_t(rows, wo_ref[cols, :]))

    live2 = jnp.where(depth_ref[0] >= 2, 1.0, 0.0).astype(f32)
    live3 = jnp.where(depth_ref[0] >= 3, 1.0, 0.0).astype(f32)

    def keys_at(c):
        return kbuf[c].reshape(CHUNK, HD)

    def values_at(c):
        return vbuf[c].reshape(CHUNK, HD)

    shape = (ROWS, CHUNK)

    def scores(query, c):
        s = dot_t(query, keys_at(c))
        sbuf[c] = s
        best_ref[...] = jnp.maximum(best_ref[...], lane_max(s))

    def own_scores(query):
        s = dot_t(query, keys_at(y))
        token = lax.broadcasted_iota(jnp.int32, shape, 0) % TOK + z * TOK
        s = jnp.where(lax.broadcasted_iota(jnp.int32, shape, 1) <= token, s, very_low)
        sbuf[y] = s
        best_ref[...] = lane_max(s)

    def step_scores(query, step):
        @pl.when(y >= step)
        def _():
            scores(query, y - step)

        if step < 4:
            @pl.when(y + step >= N_Y)
            def _():
                scores(query, y + step - N_Y)

    def weigh(level, factor):
        best = jnp.max(best_ref[...], axis=1, keepdims=True)
        if factor is not None:
            best = best * factor

        def turn(c, carry):
            total, accum = carry
            s = sbuf[c]
            if factor is not None:
                s = s * factor
            p = jnp.exp2(s - best)
            total = total + lane_fold(p)
            p = p.astype(bf16)
            pbuf[level, c] = p
            return total, accum + dot(p, values_at(c))

        total, accum = lax.fori_loop(
            0, y + 1, turn, (jnp.zeros((ROWS, 128), f32), jnp.zeros((ROWS, HD), f32))
        )
        share = 1.0 / jnp.sum(total, axis=1, keepdims=True)
        return (accum * share).astype(bf16), share

    def backward(level, grad_att, attended, share):
        delta = jnp.sum(grad_att.astype(f32) * attended.astype(f32), axis=1, keepdims=True)

        def turn(c, accum):
            dprobs = dot_t(grad_att, values_at(c))
            ds = (pbuf[level, c].astype(f32) * (dprobs - delta)).astype(bf16)
            return accum + dot(ds, keys_at(c))

        accum = lax.fori_loop(0, y + 1, turn, jnp.zeros((ROWS, HD), f32))
        return (accum * (share * SCALE)).astype(bf16)

    def rows_product(which, weight):
        total = dot(rows_recv[which, 0], weight(0))
        for h in range(1, N_MP):
            total = total + dot(rows_recv[which, h], weight(h))
        return total

    def out_product(which):
        return rows_product(which, lambda h: wo_ref[h * 256 : (h + 1) * 256, :])

    def tile_product(which, buf):
        return rows_product(which, lambda h: buf[h].reshape(256, 256))

    def query_product(which):
        total = dot_t(rows_recv[which, 0], wq_ref[:, 0:256])
        for h in range(1, N_MP):
            total = total + dot_t(rows_recv[which, h], wq_ref[:, h * 256 : (h + 1) * 256])
        return total

    def inverse_of(which):
        return lax.rsqrt(stat_sum(which) * (1.0 / D) + epsilon)

    def twice(a):
        return jnp.concatenate([a, a], axis=0)

    first_start(0, k_hbm, v_hbm, kbuf, vbuf)
    for load in loads[2:5]:
        load.wait()
    x_f = x_ref[...].astype(f32)
    project_query(0, x_f)
    stat_start(0, row_stat(x_f * x_f))
    kv_inject(0)
    kv_inject(1)
    for load in loads[5:]:
        load.wait()
    project_grad(1, cot_ref[...])
    kv_inject(2)
    kv_inject(3)

    gain = gain_ref[...]
    tile_f = dot((wo_ref[pl.ds(pl.multiple_of(seq * TILE, TILE), TILE), :].astype(f32) * gain).astype(bf16), wq_ref[...])
    group = wq_ref[:, pl.ds(pl.multiple_of(seq // 4 * 128, 128), 128)]
    turned[...] = (group.astype(f32).T * gain).astype(bf16)
    tile_b = dot_t(turned[pl.ds(pl.multiple_of(seq % 4 * TILE, TILE), TILE), :], wo_ref[...])
    for h in range(N_MP):
        tile_buf[h, 0] = tile_f[:, h * 256 : (h + 1) * 256].astype(bf16)
        tile_buf[h, 1] = tile_b[:, h * 256 : (h + 1) * 256].astype(bf16)
    for k in ORDER:
        peer = (me + k) % N_MP
        send(tile_buf.at[peer], tile_recv.at[me], tile_send_sem.at[k], tile_recv_sem.at[me], at(y, z, peer))

    ring_turn(kv, 4, kv_sems, 0)
    ring_turn(kv, 4, kv_sems, 1)
    raw2 = part_sum(0)
    inverse2 = inverse_of(0)
    query2 = (raw2 * (twice(spread(inverse2)) * (SCALE * LOG2E))).astype(bf16)
    own_scores(query2)
    ring_turn(kv, 4, kv_sems, 2)
    ring_turn(kv, 4, kv_sems, 3)
    step_scores(query2, 1)
    ring_turn(kv, 4, kv_sems, 4)
    ring_turn(kv, 4, kv_sems, 5)
    tile = tile_buf[me].astype(f32)
    for k in ORDER:
        peer = (me + k) % N_MP
        arrived(tile_recv.at[peer], tile_send_sem.at[0], tile_recv_sem.at[peer], at(y, z, peer))
        tile = tile + tile_recv[peer].astype(f32)
    mf_buf[y, z] = tile[0].astype(bf16)
    mb_buf[y, z] = tile[1].astype(bf16)
    first_start(1, mf_buf.at[y, z], mb_buf.at[y, z], mf_buf, mb_buf)
    ring_turn(kv, 4, kv_sems, 6)
    ring_turn(kv, 4, kv_sems, 7)
    step_scores(query2, 2)
    for index in range(8, 12):
        ring_turn(kv, 4, kv_sems, index)
    for k in NEAR:
        first_wait_y(1, mf_buf, (z + k) % N_Z)
        first_wait_z(1, mb_buf, (y + k) % N_Y)
    for part in range(2):
        for stream in range(4):
            ring_start(tiles, 2, tile_sems, stream, (1, part))
    step_scores(query2, 3)
    ring_turn(kv, 4, kv_sems, 12)
    ring_turn(kv, 4, kv_sems, 13)
    step_scores(query2, 4)

    attended2, share2 = weigh(0, None)
    rows_start(0, side(attended2))
    for index in range(7):
        ring_turn(tiles, 2, tile_sems, index)
        if index == 3:
            grad_att3 = part_sum(1)
    rows_wait(0)
    x3 = (x_ref[...].astype(f32) + live2 * out_product(0)).astype(bf16)
    state3[...] = x3
    x3_f = x3.astype(f32)
    stat_start(1, row_stat(x3_f * x3_f))

    raw3 = raw2 + stack(live2 * tile_product(0, mf_buf))
    query3 = (raw3 * (SCALE * LOG2E)).astype(bf16)
    own_scores(query3)

    def score_turn(c, carry):
        scores(query3, c)
        return carry

    lax.fori_loop(0, y, score_turn, 0)
    project_grad(2, x3)
    inverse3 = inverse_of(1)
    factor3 = twice(spread(inverse3))[:, :1]
    attended3, share3 = weigh(1, factor3)
    rows_start(1, side(attended3))
    grad_query3 = backward(1, (grad_att3 * live3).astype(bf16), attended3, share3)
    rows_start(2, side(grad_query3))
    stat_start(2, row_stat(side(grad_query3.astype(f32) * raw3)))

    rows_wait(1)
    mixed_ref[...] = (state3[...].astype(f32) + live3 * out_product(1)).astype(bf16)

    state_part = part_sum(2)
    inner3 = stat_sum(2)
    coef3 = inverse3 * inverse3 * inverse3 * inner3 * (1.0 / D)
    rows_wait(2)
    through = stack(tile_product(2, mb_buf))
    grad_att2 = live2 * (grad_att3 + twice(spread(inverse3)) * through - twice(spread(coef3)) * state_part)
    grad_query2 = backward(0, grad_att2.astype(bf16), attended2, share2)
    rows_start(3, side(grad_query2))
    stat_start(3, row_stat(side(grad_query2.astype(f32) * raw2)))

    def grad_input(which, state, inverse, coef, grad_f):
        scaled = query_product(which) * gain_ref[...]
        inv = widen(spread(inverse), PART // 128)
        return (grad_f + inv * scaled - state.astype(f32) * widen(spread(coef), PART // 128)).astype(bf16)

    grad3 = grad_input(2, state3[...], inverse3, coef3, cot_ref[...].astype(f32))
    inner2 = stat_sum(3)
    coef2 = inverse2 * inverse2 * inverse2 * inner2 * (1.0 / D)
    rows_wait(3)
    grad_ref[...] = grad_input(3, x_ref[...], inverse2, coef2, grad3.astype(f32))

    for copy in pending:
        copy.wait_send()


def shards(hidden, keys, values, norm_gain, w_query, w_out, depth, cotangent):
    any_spec = pl.BlockSpec(memory_space=pl.ANY)
    vmem_spec = pl.BlockSpec(memory_space=pltpu.VMEM)
    sem = pltpu.SemaphoreType.DMA
    out = jax.ShapeDtypeStruct((TOK, PART), bf16)
    return pl.pallas_call(
        kernel,
        out_shape=(out, out),
        in_specs=[any_spec] * 6 + [pl.BlockSpec(memory_space=pltpu.SMEM), any_spec],
        out_specs=(vmem_spec, vmem_spec),
        scratch_shapes=[
            pltpu.VMEM((TOK, PART), bf16),
            pltpu.VMEM((1, PART), f32),
            pltpu.VMEM((PART, HEADS), bf16),
            pltpu.VMEM((HEADS, PART), bf16),
            pltpu.VMEM((TOK, PART), bf16),
            pltpu.VMEM((N_Y, N_Z, TOK, HD), bf16),
            pltpu.VMEM((N_Y, N_Z, TOK, HD), bf16),
            pltpu.VMEM((N_Y, ROWS, CHUNK), f32),
            pltpu.VMEM((2, N_Y, ROWS, CHUNK), bf16),
            pltpu.VMEM((ROWS, 128), f32),
            pltpu.VMEM((3, HEADS, HD), bf16),
            pltpu.VMEM((3, N_MP, ROWS, HD), bf16),
            pltpu.VMEM((4, 8, TOK), f32),
            pltpu.VMEM((4, N_MP, 8, TOK), f32),
            pltpu.VMEM((4, TOK, ROWS), bf16),
            pltpu.VMEM((4, N_MP, TOK, ROWS), bf16),
            pltpu.VMEM((128, PART), bf16),
            pltpu.VMEM((N_MP, 2, TILE, ROWS), bf16),
            pltpu.VMEM((N_MP, 2, TILE, ROWS), bf16),
            pltpu.VMEM((N_Y, N_Z, TILE, ROWS), bf16),
            pltpu.VMEM((N_Y, N_Z, TILE, ROWS), bf16),
            pltpu.VMEM((TOK, PART), bf16),
            sem((7,)),
            sem((2, 2, 8)), sem((2, 2, 8)),
            sem((4, 14)), sem((4, 14)), sem((4, 7)), sem((4, 7)),
            sem((3, 8)), sem((3, 8)), sem((4, 8)), sem((4, 8)), sem((4, 8)), sem((4, 8)),
            sem((8,)), sem((8,)),
        ],
        compiler_params=pltpu.CompilerParams(
            collective_id=0, has_side_effects=True, vmem_limit_bytes=60 * 1024 * 1024
        ),
        name="recursion",
    )(hidden, keys, values, norm_gain.reshape(1, PART), w_query, w_out, depth, cotangent)


def solution(mesh):
    return jax.shard_map(
        shards,
        mesh=mesh,
        in_specs=(
            P("seq", "mp"),
            P("seq", "mp"),
            P("seq", "mp"),
            P("mp"),
            P("mp", None),
            P(None, "mp"),
            P("seq"),
            P("seq", "mp"),
        ),
        out_specs=(P("seq", "mp"), P("seq", "mp")),
        check_vma=False,
    )
```

```python
import jax
import jax.numpy as jnp
from jax import lax
from jax.experimental import pallas as pl
from jax.experimental.pallas import tpu as pltpu
from jax.sharding import PartitionSpec as P

D = 4096
HD = 128
N_MP = 8
N_Y = 8
N_Z = 8
TOK = 128
ROWS = 2 * TOK
PART = D // N_MP
HEADS = 2048
TILE = HEADS // (N_Y * N_Z)
CHUNK = N_Z * TOK
epsilon = 1e-05
very_low = -1e30
LOG2E = 1.4426950408889634
SCALE = HD ** (-0.5)

MESH = pl.DeviceIdType.MESH
f32 = jnp.float32
bf16 = jnp.bfloat16
ORDER = (4, 3, 5, 2, 6, 1, 7)
NEAR = (1, 7, 2, 6, 3, 5, 4)


def dot_t(a, b):
    return lax.dot_general(a, b, (((1,), (1,)), ((), ())), preferred_element_type=f32)


def dot(a, b):
    return jnp.dot(a, b, preferred_element_type=f32)


def lane_fold(a):
    out = a[:, :128]
    for i in range(1, a.shape[1] // 128):
        out = out + a[:, i * 128 : (i + 1) * 128]
    return out


def lane_max(a):
    out = a[:, :128]
    for i in range(1, a.shape[1] // 128):
        out = jnp.maximum(out, a[:, i * 128 : (i + 1) * 128])
    return out


def row_stat(a):
    return jnp.broadcast_to(jnp.sum(lane_fold(a).T, axis=0, keepdims=True), (8, TOK))


def spread(row):
    return jnp.broadcast_to(row[0:1, :], (TOK, TOK)).T


def widen(a, times):
    return jnp.concatenate([a] * times, axis=1)


def side(a):
    return jnp.concatenate([a[:TOK], a[TOK:]], axis=1)


def stack(a):
    return jnp.concatenate([a[:, :HD], a[:, HD:]], axis=0)


def ring_units(parts, sense):
    whole = [(step, part) for step in (1, 2, 3) for part in range(parts)]
    half = range(parts // 2) if sense > 0 else range(parts // 2, parts)
    return whole + [(4, part) for part in half]


def kernel(
    x_hbm, k_hbm, v_hbm, gain_hbm, wq_hbm, wo_hbm, depth_ref, cot_hbm,
    mixed_ref, grad_ref,
    x_ref, gain_ref, wq_ref, wo_ref, cot_ref,
    kbuf, vbuf, sbuf, pbuf, best_ref,
    part_buf, part_recv, stat_buf, stat_recv,
    rows_recv,
    turned, tile_buf, tile_recv, tiles,
    state3,
    load_sem, first_send, first_recv,
    ring_send, ring_recv, tile_ring_send, tile_ring_recv,
    part_send_sem, part_recv_sem, stat_send_sem, stat_recv_sem, rows_send_sem, rows_recv_sem,
    tile_send_sem, tile_recv_sem,
):
    seq = lax.axis_index("seq")
    me = lax.axis_index("mp")
    y = seq // N_Z
    z = seq % N_Z
    pending = []

    def at(yy, zz, mm):
        return (yy * N_Z + zz, mm)

    loads = [
        pltpu.make_async_copy(k_hbm, kbuf.at[y, z], load_sem.at[0]),
        pltpu.make_async_copy(v_hbm, vbuf.at[y, z], load_sem.at[1]),
        pltpu.make_async_copy(x_hbm, x_ref, load_sem.at[2]),
        pltpu.make_async_copy(gain_hbm, gain_ref, load_sem.at[3]),
        pltpu.make_async_copy(wq_hbm, wq_ref, load_sem.at[4]),
        pltpu.make_async_copy(cot_hbm, cot_ref, load_sem.at[5]),
        pltpu.make_async_copy(wo_hbm, wo_ref, load_sem.at[6]),
    ]
    for load in loads:
        load.start()

    targets = (at(y, (z + 1) % N_Z, me), at(y, (z + 7) % N_Z, me), at((y + 1) % N_Y, z, me), at((y + 7) % N_Y, z, me))
    barrier = pltpu.get_barrier_semaphore()
    for target in targets + tuple(at(y, z, (me + k) % N_MP) for k in range(1, 8)):
        pl.semaphore_signal(barrier, inc=1, device_id=target, device_id_type=MESH)
    pl.semaphore_wait(barrier, 11)

    def send(src, dst, send_sem, recv_sem, target):
        copy = pltpu.make_async_remote_copy(
            src_ref=src, dst_ref=dst, send_sem=send_sem, recv_sem=recv_sem,
            device_id=target, device_id_type=MESH,
        )
        copy.start()
        pending.append(copy)

    def arrived(dst, send_sem, recv_sem, source):
        pltpu.make_async_remote_copy(
            src_ref=dst, dst_ref=dst, send_sem=send_sem, recv_sem=recv_sem,
            device_id=source, device_id_type=MESH,
        ).wait_recv()

    def first_piece(gather, stream, step, shift):
        bufs = gather[0]
        away = (1 if stream % 2 == 0 else -1) * (step - shift)
        if stream < 2:
            block = bufs[0].at[y, (z + 8 - away) % N_Z]
        else:
            block = bufs[1].at[(y + 8 - away) % N_Y, z]
        if step < 4:
            return block
        half = bufs[0].shape[2] // 2
        return block.at[pl.ds(stream % 2 * half, half)]

    def first_start(gather, step):
        for stream in range(4):
            ref = first_piece(gather, stream, step, 1)
            send(ref, ref, gather[2].at[stream, step], gather[3].at[stream, step], targets[stream])

    def first_turn(gather, step):
        for stream in range(4):
            ref = first_piece(gather, stream, step, 0)
            arrived(ref, gather[2].at[stream, step], gather[3].at[stream, step], targets[stream ^ 1])
        if step < 4:
            first_start(gather, step + 1)

    def piece(gather, stream, unit, shift):
        bufs, parts = gather[0], gather[1]
        away = (1 if stream % 2 == 0 else -1) * (unit[0] - shift)
        width = 8 // parts
        mine, across = (z, y) if stream < 2 else (y, z)
        if parts == 4:
            toward = 2 * (mine % 2) - 1
            turn = (0, toward, -toward, 2)[unit[1]]
        else:
            turn = unit[1]
        span = pl.ds((mine // width + parts + turn) % parts * width, width)
        if stream < 2:
            return bufs[0].at[(across + 8 - away) % N_Y, span]
        return bufs[1].at[span, (across + 8 - away) % N_Z]

    def ring_start(gather, stream, unit):
        index = ring_units(gather[1], 1 if stream % 2 == 0 else -1).index(unit)
        ref = piece(gather, stream, unit, 1)
        send(ref, ref, gather[4].at[stream, index], gather[5].at[stream, index], targets[stream ^ 2])

    def inject(gather, part):
        for stream in range(4):
            ring_start(gather, stream, (1, part))

    def ring_turn(gather, index):
        for stream in range(4):
            units = ring_units(gather[1], 1 if stream % 2 == 0 else -1)
            step, part = units[index]
            ref = piece(gather, stream, (step, part), 0)
            arrived(ref, gather[4].at[stream, index], gather[5].at[stream, index], targets[stream ^ 3])
            if (step + 1, part) in units:
                ring_start(gather, stream, (step + 1, part))

    kv = ((kbuf, vbuf), 4, first_send.at[0], first_recv.at[0], ring_send, ring_recv)
    tile_f = ((tiles.at[0], tiles.at[1]), 2, first_send.at[1], first_recv.at[1], tile_ring_send.at[0], tile_ring_recv.at[0])
    tile_b = ((tiles.at[2], tiles.at[3]), 2, first_send.at[2], first_recv.at[2], tile_ring_send.at[1], tile_ring_recv.at[1])

    def part_send(which, peer, k):
        send(
            part_buf.at[which, pl.ds(pl.multiple_of(peer * ROWS, ROWS), ROWS)],
            part_recv.at[which, me],
            part_send_sem.at[which, k], part_recv_sem.at[which, me], at(y, z, peer),
        )

    def part_sum(which):
        total = part_buf[which, pl.ds(pl.multiple_of(me * ROWS, ROWS), ROWS)].astype(f32)
        for k in ORDER:
            peer = (me + k) % N_MP
            arrived(part_recv.at[which, peer], part_send_sem.at[which, 0], part_recv_sem.at[which, peer], at(y, z, peer))
            total = total + part_recv[which, peer].astype(f32)
        return total

    def stat_start(which, row):
        stat_buf[which] = row
        for k in ORDER:
            peer = (me + k) % N_MP
            send(
                stat_buf.at[which], stat_recv.at[which, me],
                stat_send_sem.at[which, k], stat_recv_sem.at[which, me], at(y, z, peer),
            )

    def stat_sum(which):
        total = stat_buf[which]
        for k in ORDER:
            peer = (me + k) % N_MP
            arrived(stat_recv.at[which, peer], stat_send_sem.at[which, 0], stat_recv_sem.at[which, peer], at(y, z, peer))
            total = total + stat_recv[which, peer]
        return total

    sibling = me + 1 - 2 * (me % 2)

    def rows_send(which, src, k, slot, target):
        send(
            src, rows_recv.at[which, slot], rows_send_sem.at[which, k], rows_recv_sem.at[which, slot], at(y, z, target)
        )

    def rows_start(which, rows):
        rows_recv[which, me] = rows
        for k in (4, 2, 6):
            rows_send(which, rows_recv.at[which, me], k, me, (me + k) % N_MP)
        rows_send(which, rows_recv.at[which, me], 0, me, sibling)

    def rows_wait(which, source):
        arrived(
            rows_recv.at[which, source], rows_send_sem.at[which, 0], rows_recv_sem.at[which, source], at(y, z, source)
        )

    def rows_forward(which):
        for k in (2, 6, 4):
            source = (me + k) % N_MP
            rows_wait(which, source)
            rows_send(which, rows_recv.at[which, source], k + 1, source, sibling)

    def rows_product(which, product, wait=True):
        total = product(rows_recv[which, me], me)
        for k in (2, 6, 4):
            source = (me + k) % N_MP
            total = total + product(rows_recv[which, source], source)
        for k in (0, 2, 6, 4):
            source = (sibling + k) % N_MP
            if wait:
                rows_wait(which, source)
            total = total + product(rows_recv[which, source], source)
        return total

    def drain():
        for copy in pending:
            copy.wait_send()
        pending.clear()

    def project(which, product, peers=ORDER + (0,)):
        for k in peers:
            peer = (me + k) % N_MP
            cols = product(pl.ds(pl.multiple_of(peer * 256, 256), 256)).astype(bf16)
            part_buf[which, pl.ds(pl.multiple_of(peer * ROWS, ROWS), ROWS)] = stack(cols)
            if k:
                part_send(which, peer, k)

    def query_cols(rows):
        return lambda cols: dot(rows, wq_ref[:, cols])

    def grad_cols(rows):
        return lambda cols: dot_t(rows, wo_ref[cols, :])

    live2 = jnp.where(depth_ref[0] >= 2, 1.0, 0.0).astype(f32)
    live3 = jnp.where(depth_ref[0] >= 3, 1.0, 0.0).astype(f32)

    def keys_at(c):
        return kbuf[c].reshape(CHUNK, HD)

    def values_at(c):
        return vbuf[c].reshape(CHUNK, HD)

    shape = (ROWS, CHUNK)

    def scores(query, c):
        s = dot_t(query, keys_at(c))
        sbuf[c] = s
        best_ref[...] = jnp.maximum(best_ref[...], lane_max(s))

    def own_scores(query):
        s = dot_t(query, keys_at(y))
        token = lax.broadcasted_iota(jnp.int32, shape, 0) % TOK + z * TOK
        s = jnp.where(lax.broadcasted_iota(jnp.int32, shape, 1) <= token, s, very_low)
        sbuf[y] = s
        best_ref[...] = lane_max(s)

    def step_scores(query, step):
        @pl.when(y >= step)
        def _():
            scores(query, y - step)

        if step < 4:
            @pl.when(y + step >= N_Y)
            def _():
                scores(query, y + step - N_Y)

    def weigh(level, factor):
        best = jnp.max(best_ref[...], axis=1, keepdims=True)
        if factor is not None:
            best = best * factor

        def weights(c):
            s = sbuf[c]
            if factor is not None:
                s = s * factor
            p = jnp.exp2(s - best)
            total = lane_fold(p)
            p = p.astype(bf16)
            pbuf[level, c] = p
            return total, dot(p, values_at(c))

        def two(i, carry):
            first, second = weights(2 * i), weights(2 * i + 1)
            return carry[0] + first[0] + second[0], carry[1] + first[1] + second[1]

        def one(c, carry):
            first = weights(c)
            return carry[0] + first[0], carry[1] + first[1]

        count = y + 1
        carry = lax.fori_loop(0, count // 2, two, (jnp.zeros((ROWS, 128), f32), jnp.zeros((ROWS, HD), f32)))
        total, accum = lax.fori_loop(count // 2 * 2, count, one, carry)
        share = 1.0 / jnp.sum(total, axis=1, keepdims=True)
        return (accum * share).astype(bf16), share

    def backward(level, grad_att, attended, share):
        delta = jnp.sum(grad_att.astype(f32) * attended.astype(f32), axis=1, keepdims=True)

        def turn(c, accum):
            dprobs = dot_t(grad_att, values_at(c))
            ds = (pbuf[level, c].astype(f32) * (dprobs - delta)).astype(bf16)
            return accum + dot(ds, keys_at(c))

        accum = lax.fori_loop(0, y + 1, turn, jnp.zeros((ROWS, HD), f32))
        return (accum * (share * SCALE)).astype(bf16)

    def head_cols(j):
        return pl.ds(pl.multiple_of(j * ROWS, ROWS), ROWS)

    def out_product(rows, j):
        return dot(rows, wo_ref[head_cols(j), :])

    def query_product(rows, j):
        return dot_t(rows, wq_ref[:, head_cols(j)])

    def tile_product(first):
        def product(rows, j):
            return jnp.concatenate(
                [dot(rows, tiles[first + half, j].reshape(ROWS, HD)) for half in range(2)], axis=0
            )
        return product

    def inverse_of(which):
        return lax.rsqrt(stat_sum(which) * (1.0 / D) + epsilon)

    def twice(a):
        return jnp.concatenate([a, a], axis=0)

    loads[0].wait()
    loads[1].wait()
    first_start(kv, 1)
    for load in loads[2:5]:
        load.wait()
    x_f = x_ref[...].astype(f32)
    gain = gain_ref[...]
    project(0, query_cols((x_f * gain).astype(bf16)))
    stat_start(0, row_stat(x_f * x_f))
    first_turn(kv, 1)
    inject(kv, 0)
    for load in loads[5:]:
        load.wait()
    cot = cot_ref[...]
    project(1, grad_cols(cot), ORDER[:3])
    first_turn(kv, 2)
    inject(kv, 1)
    project(1, grad_cols(cot), ORDER[3:] + (0,))
    first_turn(kv, 3)
    inject(kv, 2)
    rows_f = dot((wo_ref[pl.ds(pl.multiple_of(seq * TILE, TILE), TILE), :].astype(f32) * gain).astype(bf16), wq_ref[...])
    ring_turn(kv, 0)
    first_turn(kv, 4)
    inject(kv, 3)
    group = wq_ref[:, pl.ds(pl.multiple_of(seq // 4 * 128, 128), 128)]
    turned[...] = (group.astype(f32).T * gain).astype(bf16)
    rows_b = dot_t(turned[pl.ds(pl.multiple_of(seq % 4 * TILE, TILE), TILE), :], wo_ref[...])
    ring_turn(kv, 1)
    for h in range(N_MP):
        for i, rows in enumerate((rows_f, rows_b)):
            for half in range(2):
                start = h * ROWS + half * HD
                tile_buf[h, 2 * i + half] = rows[:, start : start + HD].astype(bf16)
    for k in ORDER:
        peer = (me + k) % N_MP
        send(tile_buf.at[peer], tile_recv.at[me], tile_send_sem.at[k], tile_recv_sem.at[me], at(y, z, peer))
    ring_turn(kv, 2)
    raw2 = part_sum(0)
    inverse2 = inverse_of(0)
    query2 = (raw2 * (twice(spread(inverse2)) * (SCALE * LOG2E))).astype(bf16)
    ring_turn(kv, 3)
    own_scores(query2)
    ring_turn(kv, 4)
    step_scores(query2, 1)
    ring_turn(kv, 5)
    tile = tile_buf[me].astype(f32)
    for k in ORDER:
        peer = (me + k) % N_MP
        arrived(tile_recv.at[peer], tile_send_sem.at[0], tile_recv_sem.at[peer], at(y, z, peer))
        tile = tile + tile_recv[peer].astype(f32)
    for i in range(4):
        tiles[i, y, z] = tile[i].astype(bf16)
    first_start(tile_f, 1)
    ring_turn(kv, 6)
    grad_att3 = part_sum(1)
    ring_turn(kv, 7)
    first_turn(tile_f, 1)
    first_start(tile_b, 1)
    step_scores(query2, 2)
    ring_turn(kv, 8)
    first_turn(tile_f, 2)
    ring_turn(kv, 9)
    first_turn(tile_b, 1)
    ring_turn(kv, 10)
    first_turn(tile_f, 3)
    inject(tile_f, 0)
    ring_turn(kv, 11)
    first_turn(tile_f, 4)
    inject(tile_f, 1)
    step_scores(query2, 3)
    ring_turn(kv, 12)
    ring_turn(kv, 13)
    step_scores(query2, 4)

    ring_turn(tile_f, 0)
    ring_turn(tile_f, 1)
    attended2, share2 = weigh(0, None)
    rows_start(0, side(attended2))
    ring_turn(tile_f, 2)
    ring_turn(tile_f, 3)
    first_turn(tile_b, 2)
    drain()
    rows_forward(0)
    ring_turn(tile_f, 4)
    first_turn(tile_b, 3)
    inject(tile_b, 0)
    x3 = (x_ref[...].astype(f32) + live2 * rows_product(0, out_product)).astype(bf16)
    state3[...] = x3
    x3_f = x3.astype(f32)
    stat_start(1, row_stat(x3_f * x3_f))

    project(2, grad_cols(x3))
    first_turn(tile_b, 4)
    inject(tile_b, 1)
    ring_turn(tile_f, 5)
    ring_turn(tile_f, 6)
    raw3 = raw2 + live2 * rows_product(0, tile_product(0), wait=False)
    query3 = (raw3 * (SCALE * LOG2E)).astype(bf16)
    own_scores(query3)

    def score_turn(c, carry):
        scores(query3, c)
        return carry

    lax.fori_loop(0, y, score_turn, 0)
    ring_turn(tile_b, 0)
    ring_turn(tile_b, 1)
    inverse3 = inverse_of(1)
    factor3 = twice(spread(inverse3))[:, :1]
    attended3, share3 = weigh(1, factor3)
    ring_turn(tile_b, 2)
    ring_turn(tile_b, 3)
    grad_query3 = backward(1, (grad_att3 * live3).astype(bf16), attended3, share3)
    rows_start(2, side(grad_query3))
    stat_start(2, row_stat(side(grad_query3.astype(f32) * raw3)))
    ring_turn(tile_b, 4)
    ring_turn(tile_b, 5)
    drain()
    rows_forward(2)
    ring_turn(tile_b, 6)
    state_part = part_sum(2)

    through = rows_product(2, tile_product(2))
    inner3 = stat_sum(2)
    coef3 = inverse3 * inverse3 * inverse3 * inner3 * (1.0 / D)
    grad_att2 = live2 * (grad_att3 + twice(spread(inverse3)) * through - twice(spread(coef3)) * state_part)
    rows_start(1, side(attended3))
    grad_query2 = backward(0, grad_att2.astype(bf16), attended2, share2)
    rows_start(3, side(grad_query2))
    stat_start(3, row_stat(side(grad_query2.astype(f32) * raw2)))
    rows_forward(1)
    mixed_ref[...] = (state3[...].astype(f32) + live3 * rows_product(1, out_product)).astype(bf16)

    def grad_input(which, wait, state, inverse, coef, grad_f):
        inv = widen(spread(inverse), PART // 128)
        rest = grad_f - state.astype(f32) * widen(spread(coef), PART // 128)
        return (rest + inv * gain * rows_product(which, query_product, wait)).astype(bf16)

    grad3 = grad_input(2, False, state3[...], inverse3, coef3, cot_ref[...].astype(f32))
    drain()
    rows_forward(3)
    inner2 = stat_sum(3)
    coef2 = inverse2 * inverse2 * inverse2 * inner2 * (1.0 / D)
    grad_ref[...] = grad_input(3, True, x_ref[...], inverse2, coef2, grad3.astype(f32))
    drain()


def shards(hidden, keys, values, norm_gain, w_query, w_out, depth, cotangent):
    any_spec = pl.BlockSpec(memory_space=pl.ANY)
    vmem_spec = pl.BlockSpec(memory_space=pltpu.VMEM)
    sem = pltpu.SemaphoreType.DMA
    out = jax.ShapeDtypeStruct((TOK, PART), bf16)
    return pl.pallas_call(
        kernel,
        out_shape=(out, out),
        in_specs=[any_spec] * 6 + [pl.BlockSpec(memory_space=pltpu.SMEM), any_spec],
        out_specs=(vmem_spec, vmem_spec),
        scratch_shapes=[
            pltpu.VMEM((TOK, PART), bf16),
            pltpu.VMEM((1, PART), f32),
            pltpu.VMEM((PART, HEADS), bf16),
            pltpu.VMEM((HEADS, PART), bf16),
            pltpu.VMEM((TOK, PART), bf16),
            pltpu.VMEM((N_Y, N_Z, TOK, HD), bf16),
            pltpu.VMEM((N_Y, N_Z, TOK, HD), bf16),
            pltpu.VMEM((N_Y, ROWS, CHUNK), f32),
            pltpu.VMEM((2, N_Y, ROWS, CHUNK), bf16),
            pltpu.VMEM((ROWS, 128), f32),
            pltpu.VMEM((3, HEADS, HD), bf16),
            pltpu.VMEM((3, N_MP, ROWS, HD), bf16),
            pltpu.VMEM((4, 8, TOK), f32),
            pltpu.VMEM((4, N_MP, 8, TOK), f32),
            pltpu.VMEM((4, N_MP, TOK, ROWS), bf16),
            pltpu.VMEM((128, PART), bf16),
            pltpu.VMEM((N_MP, 4, TILE, HD), bf16),
            pltpu.VMEM((N_MP, 4, TILE, HD), bf16),
            pltpu.VMEM((4, N_Y, N_Z, TILE, HD), bf16),
            pltpu.VMEM((TOK, PART), bf16),
            sem((7,)),
            sem((3, 4, 5)), sem((3, 4, 5)),
            sem((4, 14)), sem((4, 14)), sem((2, 4, 7)), sem((2, 4, 7)),
            sem((3, 8)), sem((3, 8)), sem((4, 8)), sem((4, 8)), sem((4, 8)), sem((4, 8)),
            sem((8,)), sem((8,)),
        ],
        compiler_params=pltpu.CompilerParams(
            collective_id=0, has_side_effects=True, vmem_limit_bytes=60 * 1024 * 1024
        ),
        name="recursion",
    )(hidden, keys, values, norm_gain.reshape(1, PART), w_query, w_out, depth, cotangent)


def solution(mesh):
    return jax.shard_map(
        shards,
        mesh=mesh,
        in_specs=(
            P("seq", "mp"),
            P("seq", "mp"),
            P("seq", "mp"),
            P("mp"),
            P("mp", None),
            P(None, "mp"),
            P("seq"),
            P("seq", "mp"),
        ),
        out_specs=(P("seq", "mp"), P("seq", "mp")),
        check_vma=False,
    )
```

```python
import jax
import jax.numpy as jnp
from jax import lax
from jax.experimental import pallas as pl
from jax.experimental.pallas import tpu as pltpu
from jax.sharding import PartitionSpec as P

D = 4096
HD = 128
N_MP = 8
N_Y = 8
N_Z = 8
TOK = 128
ROWS = 2 * TOK
PART = D // N_MP
HEADS = 2048
TILE = HEADS // (N_Y * N_Z)
CHUNK = N_Z * TOK
epsilon = 1e-05
very_low = -1e30
LOG2E = 1.4426950408889634
SCALE = HD ** (-0.5)

MESH = pl.DeviceIdType.MESH
f32 = jnp.float32
bf16 = jnp.bfloat16
ORDER = (4, 3, 5, 2, 6, 1, 7)
NEAR = (1, 7, 2, 6, 3, 5, 4)


def dot_t(a, b):
    return lax.dot_general(a, b, (((1,), (1,)), ((), ())), preferred_element_type=f32)


def dot(a, b):
    return jnp.dot(a, b, preferred_element_type=f32)


def lane_fold(a):
    out = a[:, :128]
    for i in range(1, a.shape[1] // 128):
        out = out + a[:, i * 128 : (i + 1) * 128]
    return out


def lane_max(a):
    out = a[:, :128]
    for i in range(1, a.shape[1] // 128):
        out = jnp.maximum(out, a[:, i * 128 : (i + 1) * 128])
    return out


def row_stat(a):
    return jnp.broadcast_to(jnp.sum(lane_fold(a).T, axis=0, keepdims=True), (8, TOK))


def spread(row):
    return jnp.broadcast_to(row[0:1, :], (TOK, TOK)).T


def widen(a, times):
    return jnp.concatenate([a] * times, axis=1)


def side(a):
    return jnp.concatenate([a[:TOK], a[TOK:]], axis=1)


def stack(a):
    return jnp.concatenate([a[:, :HD], a[:, HD:]], axis=0)


def ring_units(parts, sense):
    whole = [(step, part) for step in (1, 2, 3) for part in range(parts)]
    half = range(parts // 2) if sense > 0 else range(parts // 2, parts)
    return whole + [(4, part) for part in half]


def kernel(
    x_hbm, k_hbm, v_hbm, gain_hbm, wq_hbm, wo_hbm, depth_ref, cot_hbm,
    mixed_ref, grad_ref,
    x_ref, gain_ref, wq_ref, wo_ref, cot_ref,
    kbuf, vbuf, sbuf, pbuf, best_ref,
    part_buf, part_recv, stat_buf, stat_recv,
    rows_recv,
    turned, tile_buf, tile_recv, tiles,
    state3,
    load_sem, first_send, first_recv,
    tile_first_send, tile_first_recv,
    ring_send, ring_recv, tile_ring_send, tile_ring_recv,
    part_send_sem, part_recv_sem, stat_send_sem, stat_recv_sem, rows_send_sem, rows_recv_sem,
    tile_send_sem, tile_recv_sem,
):
    seq = lax.axis_index("seq")
    me = lax.axis_index("mp")
    y = seq // N_Z
    z = seq % N_Z
    pending = []

    def at(yy, zz, mm):
        return (yy * N_Z + zz, mm)

    loads = [
        pltpu.make_async_copy(k_hbm, kbuf.at[y, z], load_sem.at[0]),
        pltpu.make_async_copy(v_hbm, vbuf.at[y, z], load_sem.at[1]),
        pltpu.make_async_copy(x_hbm, x_ref, load_sem.at[2]),
        pltpu.make_async_copy(gain_hbm, gain_ref, load_sem.at[3]),
        pltpu.make_async_copy(wq_hbm, wq_ref, load_sem.at[4]),
        pltpu.make_async_copy(cot_hbm, cot_ref, load_sem.at[5]),
        pltpu.make_async_copy(wo_hbm, wo_ref, load_sem.at[6]),
    ]
    for load in loads:
        load.start()

    targets = (at(y, (z + 1) % N_Z, me), at(y, (z + 7) % N_Z, me), at((y + 1) % N_Y, z, me), at((y + 7) % N_Y, z, me))
    barrier = pltpu.get_barrier_semaphore()
    for k in NEAR:
        for target in (at(y, (z + k) % N_Z, me), at((y + k) % N_Y, z, me), at(y, z, (me + k) % N_MP)):
            pl.semaphore_signal(barrier, inc=1, device_id=target, device_id_type=MESH)
    pl.semaphore_wait(barrier, 21)

    def send(src, dst, send_sem, recv_sem, target):
        copy = pltpu.make_async_remote_copy(
            src_ref=src, dst_ref=dst, send_sem=send_sem, recv_sem=recv_sem,
            device_id=target, device_id_type=MESH,
        )
        copy.start()
        pending.append(copy)

    def arrived(dst, send_sem, recv_sem, source):
        pltpu.make_async_remote_copy(
            src_ref=dst, dst_ref=dst, send_sem=send_sem, recv_sem=recv_sem,
            device_id=source, device_id_type=MESH,
        ).wait_recv()

    def first_piece(gather, stream, step, shift):
        bufs = gather[0]
        away = (1 if stream % 2 == 0 else -1) * (step - shift)
        if stream < 2:
            block = bufs[0].at[y, (z + 8 - away) % N_Z]
        else:
            block = bufs[1].at[(y + 8 - away) % N_Y, z]
        if step < 4:
            return block
        half = bufs[0].shape[2] // 2
        return block.at[pl.ds(stream % 2 * half, half)]

    def first_start(gather, step):
        for stream in range(4):
            ref = first_piece(gather, stream, step, 1)
            send(ref, ref, gather[2].at[stream, step], gather[3].at[stream, step], targets[stream])

    def first_own(gather):
        first_start(gather, 1)
        two = (at(y, (z + 2) % N_Z, me), at(y, (z + 6) % N_Z, me), at((y + 2) % N_Y, z, me), at((y + 6) % N_Y, z, me))
        for stream in range(4):
            ref = first_piece(gather, stream, 2, 2)
            send(ref, ref, gather[2].at[stream, 2], gather[3].at[stream, 2], two[stream])

    def first_all(gather):
        for k in NEAR:
            for i, target in enumerate((at(y, (z + k) % N_Z, me), at((y + k) % N_Y, z, me))):
                ref = gather[0][i].at[y, z]
                send(ref, ref, gather[2].at[i, k], gather[3].at[i, (z, y)[i]], target)

    def first_all_wait(gather):
        for k in NEAR:
            for i in range(2):
                other = ((z, y)[i] + k) % 8
                where = (y, other) if i == 0 else (other, z)
                arrived(gather[0][i].at[where], gather[2].at[i, 0], gather[3].at[i, other], at(*where, me))

    def first_turn(gather, step):
        for stream in range(4):
            ref = first_piece(gather, stream, step, 0)
            arrived(ref, gather[2].at[stream, step], gather[3].at[stream, step], targets[stream ^ 1])
        if step in (2, 3):
            first_start(gather, step + 1)

    def piece(gather, stream, unit, shift):
        bufs, parts = gather[0], gather[1]
        away = (1 if stream % 2 == 0 else -1) * (unit[0] - shift)
        width = 8 // parts
        mine, across = (z, y) if stream < 2 else (y, z)
        if parts == 4:
            toward = 2 * (mine % 2) - 1
            turn = (0, toward, -toward, 2)[unit[1]]
        else:
            turn = unit[1]
        span = pl.ds((mine // width + parts + turn) % parts * width, width)
        if stream < 2:
            return bufs[0].at[(across + 8 - away) % N_Y, span]
        return bufs[1].at[span, (across + 8 - away) % N_Z]

    def ring_start(gather, stream, unit):
        index = ring_units(gather[1], 1 if stream % 2 == 0 else -1).index(unit)
        ref = piece(gather, stream, unit, 1)
        send(ref, ref, gather[4].at[stream, index], gather[5].at[stream, index], targets[stream ^ 2])

    def inject(gather, part):
        for stream in range(4):
            ring_start(gather, stream, (1, part))

    def ring_turn(gather, index):
        for stream in range(4):
            units = ring_units(gather[1], 1 if stream % 2 == 0 else -1)
            step, part = units[index]
            ref = piece(gather, stream, (step, part), 0)
            arrived(ref, gather[4].at[stream, index], gather[5].at[stream, index], targets[stream ^ 3])
            if (step + 1, part) in units:
                ring_start(gather, stream, (step + 1, part))

    kv = ((kbuf, vbuf), 4, first_send, first_recv, ring_send, ring_recv)
    tile_f = ((tiles.at[0], tiles.at[1]), 2, tile_first_send.at[0], tile_first_recv.at[0], tile_ring_send.at[0], tile_ring_recv.at[0])
    tile_b = ((tiles.at[2], tiles.at[3]), 2, tile_first_send.at[1], tile_first_recv.at[1], tile_ring_send.at[1], tile_ring_recv.at[1])

    def part_send(which, peer, k):
        send(
            part_buf.at[which, pl.ds(pl.multiple_of(peer * ROWS, ROWS), ROWS)],
            part_recv.at[which, me],
            part_send_sem.at[which, k], part_recv_sem.at[which, me], at(y, z, peer),
        )

    def part_sum(which):
        total = part_buf[which, pl.ds(pl.multiple_of(me * ROWS, ROWS), ROWS)].astype(f32)
        for k in ORDER:
            peer = (me + k) % N_MP
            arrived(part_recv.at[which, peer], part_send_sem.at[which, 0], part_recv_sem.at[which, peer], at(y, z, peer))
            total = total + part_recv[which, peer].astype(f32)
        return total

    def stat_start(which, row):
        stat_buf[which] = row
        for k in ORDER:
            peer = (me + k) % N_MP
            send(
                stat_buf.at[which], stat_recv.at[which, me],
                stat_send_sem.at[which, k], stat_recv_sem.at[which, me], at(y, z, peer),
            )

    def stat_sum(which):
        total = stat_buf[which]
        for k in ORDER:
            peer = (me + k) % N_MP
            arrived(stat_recv.at[which, peer], stat_send_sem.at[which, 0], stat_recv_sem.at[which, peer], at(y, z, peer))
            total = total + stat_recv[which, peer]
        return total

    sibling = me + 1 - 2 * (me % 2)

    def rows_send(which, src, k, slot, target):
        send(
            src, rows_recv.at[which, slot], rows_send_sem.at[which, k], rows_recv_sem.at[which, slot], at(y, z, target)
        )

    def rows_start(which, rows):
        rows_recv[which, me] = rows
        for k in (4, 2, 6):
            rows_send(which, rows_recv.at[which, me], k, me, (me + k) % N_MP)
        rows_send(which, rows_recv.at[which, me], 0, me, sibling)

    def rows_wait(which, source):
        arrived(
            rows_recv.at[which, source], rows_send_sem.at[which, 0], rows_recv_sem.at[which, source], at(y, z, source)
        )

    def rows_forward(which):
        for k in (2, 6, 4):
            source = (me + k) % N_MP
            rows_wait(which, source)
            rows_send(which, rows_recv.at[which, source], k + 1, source, sibling)

    def rows_product(which, product, wait=True):
        total = product(rows_recv[which, me], me)
        for k in (2, 6, 4):
            source = (me + k) % N_MP
            total = total + product(rows_recv[which, source], source)
        for k in (0, 2, 6, 4):
            source = (sibling + k) % N_MP
            if wait:
                rows_wait(which, source)
            total = total + product(rows_recv[which, source], source)
        return total

    def drain():
        for copy in pending:
            copy.wait_send()
        pending.clear()

    def project(which, product, peers=ORDER + (0,)):
        for k in peers:
            peer = (me + k) % N_MP
            cols = product(pl.ds(pl.multiple_of(peer * 256, 256), 256)).astype(bf16)
            part_buf[which, pl.ds(pl.multiple_of(peer * ROWS, ROWS), ROWS)] = stack(cols)
            if k:
                part_send(which, peer, k)

    def query_cols(rows):
        return lambda cols: dot(rows, wq_ref[:, cols])

    def grad_cols(rows):
        return lambda cols: dot_t(rows, wo_ref[cols, :])

    live2 = jnp.where(depth_ref[0] >= 2, 1.0, 0.0).astype(f32)
    live3 = jnp.where(depth_ref[0] >= 3, 1.0, 0.0).astype(f32)

    def keys_at(c):
        return kbuf[c].reshape(CHUNK, HD)

    def values_at(c):
        return vbuf[c].reshape(CHUNK, HD)

    shape = (ROWS, CHUNK)

    def scores(query, c):
        s = dot_t(query, keys_at(c))
        sbuf[c] = s
        best_ref[...] = jnp.maximum(best_ref[...], lane_max(s))

    def own_scores(query):
        s = dot_t(query, keys_at(y))
        token = lax.broadcasted_iota(jnp.int32, shape, 0) % TOK + z * TOK
        s = jnp.where(lax.broadcasted_iota(jnp.int32, shape, 1) <= token, s, very_low)
        sbuf[y] = s
        best_ref[...] = lane_max(s)

    def step_scores(query, step):
        @pl.when(y >= step)
        def _():
            scores(query, y - step)

        if step < 4:
            @pl.when(y + step >= N_Y)
            def _():
                scores(query, y + step - N_Y)

    def weigh(level, factor):
        best = jnp.max(best_ref[...], axis=1, keepdims=True)
        if factor is not None:
            best = best * factor

        def weights(c):
            s = sbuf[c]
            if factor is not None:
                s = s * factor
            p = jnp.exp2(s - best)
            total = lane_fold(p)
            p = p.astype(bf16)
            pbuf[level, c] = p
            return total, dot(p, values_at(c))

        def two(i, carry):
            first, second = weights(2 * i), weights(2 * i + 1)
            return carry[0] + first[0] + second[0], carry[1] + first[1] + second[1]

        def one(c, carry):
            first = weights(c)
            return carry[0] + first[0], carry[1] + first[1]

        count = y + 1
        carry = lax.fori_loop(0, count // 2, two, (jnp.zeros((ROWS, 128), f32), jnp.zeros((ROWS, HD), f32)))
        total, accum = lax.fori_loop(count // 2 * 2, count, one, carry)
        share = 1.0 / jnp.sum(total, axis=1, keepdims=True)
        return (accum * share).astype(bf16), share

    def backward(level, grad_att, attended, share):
        delta = jnp.sum(grad_att.astype(f32) * attended.astype(f32), axis=1, keepdims=True)

        def turn(c, accum):
            dprobs = dot_t(grad_att, values_at(c))
            ds = (pbuf[level, c].astype(f32) * (dprobs - delta)).astype(bf16)
            return accum + dot(ds, keys_at(c))

        accum = lax.fori_loop(0, y + 1, turn, jnp.zeros((ROWS, HD), f32))
        return (accum * (share * SCALE)).astype(bf16)

    def head_cols(j):
        return pl.ds(pl.multiple_of(j * ROWS, ROWS), ROWS)

    def out_product(rows, j):
        return dot(rows, wo_ref[head_cols(j), :])

    def query_product(rows, j):
        return dot_t(rows, wq_ref[:, head_cols(j)])

    def tile_product(first):
        def product(rows, j):
            return jnp.concatenate(
                [dot(rows, tiles[first + half, j].reshape(ROWS, HD)) for half in range(2)], axis=0
            )
        return product

    def inverse_of(which):
        return lax.rsqrt(stat_sum(which) * (1.0 / D) + epsilon)

    def twice(a):
        return jnp.concatenate([a, a], axis=0)

    loads[0].wait()
    loads[1].wait()
    first_own(kv)
    for load in loads[2:5]:
        load.wait()
    x_f = x_ref[...].astype(f32)
    gain = gain_ref[...]
    project(0, query_cols((x_f * gain).astype(bf16)))
    stat_start(0, row_stat(x_f * x_f))
    first_turn(kv, 1)
    inject(kv, 0)
    for load in loads[5:]:
        load.wait()
    cot = cot_ref[...]
    project(1, grad_cols(cot), ORDER[:3])
    first_turn(kv, 2)
    inject(kv, 1)
    project(1, grad_cols(cot), ORDER[3:] + (0,))
    first_turn(kv, 3)
    inject(kv, 2)
    rows_f = dot((wo_ref[pl.ds(pl.multiple_of(seq * TILE, TILE), TILE), :].astype(f32) * gain).astype(bf16), wq_ref[...])
    ring_turn(kv, 0)
    first_turn(kv, 4)
    inject(kv, 3)
    group = wq_ref[:, pl.ds(pl.multiple_of(seq // 4 * 128, 128), 128)]
    turned[...] = (group.astype(f32).T * gain).astype(bf16)
    rows_b = dot_t(turned[pl.ds(pl.multiple_of(seq % 4 * TILE, TILE), TILE), :], wo_ref[...])
    ring_turn(kv, 1)
    for h in range(N_MP):
        for i, rows in enumerate((rows_f, rows_b)):
            for half in range(2):
                start = h * ROWS + half * HD
                tile_buf[h, 2 * i + half] = rows[:, start : start + HD].astype(bf16)
    for k in ORDER:
        peer = (me + k) % N_MP
        send(tile_buf.at[peer], tile_recv.at[me], tile_send_sem.at[k], tile_recv_sem.at[me], at(y, z, peer))
    ring_turn(kv, 2)
    raw2 = part_sum(0)
    inverse2 = inverse_of(0)
    query2 = (raw2 * (twice(spread(inverse2)) * (SCALE * LOG2E))).astype(bf16)
    ring_turn(kv, 3)
    own_scores(query2)
    ring_turn(kv, 4)
    step_scores(query2, 1)
    ring_turn(kv, 5)
    tile = tile_buf[me].astype(f32)
    for k in ORDER:
        peer = (me + k) % N_MP
        arrived(tile_recv.at[peer], tile_send_sem.at[0], tile_recv_sem.at[peer], at(y, z, peer))
        tile = tile + tile_recv[peer].astype(f32)
    for i in range(4):
        tiles[i, y, z] = tile[i].astype(bf16)
    first_all(tile_f)
    ring_turn(kv, 6)
    grad_att3 = part_sum(1)
    ring_turn(kv, 7)
    step_scores(query2, 2)
    ring_turn(kv, 8)
    ring_turn(kv, 9)
    ring_turn(kv, 10)
    ring_turn(kv, 11)
    first_all_wait(tile_f)
    inject(tile_f, 0)
    inject(tile_f, 1)
    step_scores(query2, 3)
    ring_turn(kv, 12)
    ring_turn(kv, 13)
    step_scores(query2, 4)

    attended2, share2 = weigh(0, None)
    rows_start(0, side(attended2))
    for index in range(4):
        ring_turn(tile_f, index)
    first_all(tile_b)
    rows_forward(0)
    ring_turn(tile_f, 4)
    ring_turn(tile_f, 5)
    x3 = (x_ref[...].astype(f32) + live2 * rows_product(0, out_product)).astype(bf16)
    state3[...] = x3
    x3_f = x3.astype(f32)
    stat_start(1, row_stat(x3_f * x3_f))

    project(2, grad_cols(x3))
    ring_turn(tile_f, 6)
    first_all_wait(tile_b)
    inject(tile_b, 0)
    inject(tile_b, 1)
    raw3 = raw2 + live2 * rows_product(0, tile_product(0), wait=False)
    query3 = (raw3 * (SCALE * LOG2E)).astype(bf16)
    own_scores(query3)

    def score_turn(c, carry):
        scores(query3, c)
        return carry

    lax.fori_loop(0, y, score_turn, 0)
    ring_turn(tile_b, 0)
    ring_turn(tile_b, 1)
    inverse3 = inverse_of(1)
    factor3 = twice(spread(inverse3))[:, :1]
    attended3, share3 = weigh(1, factor3)
    ring_turn(tile_b, 2)
    ring_turn(tile_b, 3)
    grad_query3 = backward(1, (grad_att3 * live3).astype(bf16), attended3, share3)
    rows_start(2, side(grad_query3))
    stat_start(2, row_stat(side(grad_query3.astype(f32) * raw3)))
    ring_turn(tile_b, 4)
    ring_turn(tile_b, 5)
    drain()
    rows_forward(2)
    ring_turn(tile_b, 6)
    state_part = part_sum(2)

    through = rows_product(2, tile_product(2))
    inner3 = stat_sum(2)
    coef3 = inverse3 * inverse3 * inverse3 * inner3 * (1.0 / D)
    grad_att2 = live2 * (grad_att3 + twice(spread(inverse3)) * through - twice(spread(coef3)) * state_part)
    rows_start(1, side(attended3))
    grad_query2 = backward(0, grad_att2.astype(bf16), attended2, share2)
    rows_start(3, side(grad_query2))
    stat_start(3, row_stat(side(grad_query2.astype(f32) * raw2)))
    rows_forward(1)
    mixed_ref[...] = (state3[...].astype(f32) + live3 * rows_product(1, out_product)).astype(bf16)

    def grad_input(which, wait, state, inverse, coef, grad_f):
        inv = widen(spread(inverse), PART // 128)
        rest = grad_f - state.astype(f32) * widen(spread(coef), PART // 128)
        return (rest + inv * gain * rows_product(which, query_product, wait)).astype(bf16)

    grad3 = grad_input(2, False, state3[...], inverse3, coef3, cot_ref[...].astype(f32))
    drain()
    rows_forward(3)
    inner2 = stat_sum(3)
    coef2 = inverse2 * inverse2 * inverse2 * inner2 * (1.0 / D)
    grad_ref[...] = grad_input(3, True, x_ref[...], inverse2, coef2, grad3.astype(f32))
    drain()


def shards(hidden, keys, values, norm_gain, w_query, w_out, depth, cotangent):
    any_spec = pl.BlockSpec(memory_space=pl.ANY)
    vmem_spec = pl.BlockSpec(memory_space=pltpu.VMEM)
    sem = pltpu.SemaphoreType.DMA
    out = jax.ShapeDtypeStruct((TOK, PART), bf16)
    return pl.pallas_call(
        kernel,
        out_shape=(out, out),
        in_specs=[any_spec] * 6 + [pl.BlockSpec(memory_space=pltpu.SMEM), any_spec],
        out_specs=(vmem_spec, vmem_spec),
        scratch_shapes=[
            pltpu.VMEM((TOK, PART), bf16),
            pltpu.VMEM((1, PART), f32),
            pltpu.VMEM((PART, HEADS), bf16),
            pltpu.VMEM((HEADS, PART), bf16),
            pltpu.VMEM((TOK, PART), bf16),
            pltpu.VMEM((N_Y, N_Z, TOK, HD), bf16),
            pltpu.VMEM((N_Y, N_Z, TOK, HD), bf16),
            pltpu.VMEM((N_Y, ROWS, CHUNK), f32),
            pltpu.VMEM((2, N_Y, ROWS, CHUNK), bf16),
            pltpu.VMEM((ROWS, 128), f32),
            pltpu.VMEM((3, HEADS, HD), bf16),
            pltpu.VMEM((3, N_MP, ROWS, HD), bf16),
            pltpu.VMEM((4, 8, TOK), f32),
            pltpu.VMEM((4, N_MP, 8, TOK), f32),
            pltpu.VMEM((4, N_MP, TOK, ROWS), bf16),
            pltpu.VMEM((128, PART), bf16),
            pltpu.VMEM((N_MP, 4, TILE, HD), bf16),
            pltpu.VMEM((N_MP, 4, TILE, HD), bf16),
            pltpu.VMEM((4, N_Y, N_Z, TILE, HD), bf16),
            pltpu.VMEM((TOK, PART), bf16),
            sem((7,)),
            sem((4, 5)), sem((4, 5)), sem((2, 2, 8)), sem((2, 2, 8)),
            sem((4, 14)), sem((4, 14)), sem((2, 4, 7)), sem((2, 4, 7)),
            sem((3, 8)), sem((3, 8)), sem((4, 8)), sem((4, 8)), sem((4, 8)), sem((4, 8)),
            sem((8,)), sem((8,)),
        ],
        compiler_params=pltpu.CompilerParams(
            collective_id=0, has_side_effects=True, vmem_limit_bytes=60 * 1024 * 1024
        ),
        name="recursion",
    )(hidden, keys, values, norm_gain.reshape(1, PART), w_query, w_out, depth, cotangent)


def solution(mesh):
    return jax.shard_map(
        shards,
        mesh=mesh,
        in_specs=(
            P("seq", "mp"),
            P("seq", "mp"),
            P("seq", "mp"),
            P("mp"),
            P("mp", None),
            P(None, "mp"),
            P("seq"),
            P("seq", "mp"),
        ),
        out_specs=(P("seq", "mp"), P("seq", "mp")),
        check_vma=False,
    )
```

```python
import jax
import jax.numpy as jnp
from jax import lax
from jax.experimental import pallas as pl
from jax.experimental.pallas import tpu as pltpu
from jax.sharding import PartitionSpec as P

D = 4096
HD = 128
N_MP = 8
N_Y = 8
N_Z = 8
TOK = 128
ROWS = 2 * TOK
PART = D // N_MP
HEADS = 2048
TILE = HEADS // (N_Y * N_Z)
CHUNK = N_Z * TOK
epsilon = 1e-05
very_low = -1e30
LOG2E = 1.4426950408889634
SCALE = HD ** (-0.5)

MESH = pl.DeviceIdType.MESH
f32 = jnp.float32
bf16 = jnp.bfloat16
ORDER = (4, 3, 5, 2, 6, 1, 7)
NEAR = (1, 7, 2, 6, 3, 5, 4)


def dot_t(a, b):
    return lax.dot_general(a, b, (((1,), (1,)), ((), ())), preferred_element_type=f32)


def dot(a, b):
    return jnp.dot(a, b, preferred_element_type=f32)


def lane_fold(a):
    out = a[:, :128]
    for i in range(1, a.shape[1] // 128):
        out = out + a[:, i * 128 : (i + 1) * 128]
    return out


def lane_max(a):
    out = a[:, :128]
    for i in range(1, a.shape[1] // 128):
        out = jnp.maximum(out, a[:, i * 128 : (i + 1) * 128])
    return out


def row_stat(a):
    return jnp.broadcast_to(jnp.sum(lane_fold(a).T, axis=0, keepdims=True), (8, TOK))


def spread(row):
    return jnp.broadcast_to(row[0:1, :], (TOK, TOK)).T


def widen(a, times):
    return jnp.concatenate([a] * times, axis=1)


def side(a):
    return jnp.concatenate([a[:TOK], a[TOK:]], axis=1)


def stack(a):
    return jnp.concatenate([a[:, :HD], a[:, HD:]], axis=0)


def ring_units(parts, sense):
    whole = [(step, part) for step in (1, 2, 3) for part in range(parts)]
    half = range(parts // 2) if sense > 0 else range(parts // 2, parts)
    return whole + [(4, part) for part in half]


def kernel(
    x_hbm, k_hbm, v_hbm, gain_hbm, wq_hbm, wo_hbm, depth_ref, cot_hbm,
    mixed_ref, grad_ref,
    x_ref, gain_ref, wq_ref, wo_ref, cot_ref,
    kbuf, vbuf, sbuf, pbuf, best_ref,
    part_buf, part_recv, stat_buf, stat_recv,
    rows_recv,
    turned, tile_buf, tile_recv, tiles,
    state3,
    load_sem, first_send, first_recv,
    tile_first_send, tile_first_recv,
    ring_send, ring_recv, tile_ring_send, tile_ring_recv,
    part_send_sem, part_recv_sem, stat_send_sem, stat_recv_sem, rows_send_sem, rows_recv_sem,
    tile_send_sem, tile_recv_sem,
):
    seq = lax.axis_index("seq")
    me = lax.axis_index("mp")
    y = seq // N_Z
    z = seq % N_Z
    pending = []

    def at(yy, zz, mm):
        return (yy * N_Z + zz, mm)

    loads = [
        pltpu.make_async_copy(k_hbm, kbuf.at[y, z], load_sem.at[0]),
        pltpu.make_async_copy(v_hbm, vbuf.at[y, z], load_sem.at[1]),
        pltpu.make_async_copy(x_hbm, x_ref, load_sem.at[2]),
        pltpu.make_async_copy(gain_hbm, gain_ref, load_sem.at[3]),
        pltpu.make_async_copy(wq_hbm, wq_ref, load_sem.at[4]),
        pltpu.make_async_copy(cot_hbm, cot_ref, load_sem.at[5]),
        pltpu.make_async_copy(wo_hbm, wo_ref, load_sem.at[6]),
    ]
    for load in loads:
        load.start()

    targets = (at(y, (z + 1) % N_Z, me), at(y, (z + 7) % N_Z, me), at((y + 1) % N_Y, z, me), at((y + 7) % N_Y, z, me))
    barrier = pltpu.get_barrier_semaphore()
    for k in NEAR:
        for target in (at(y, (z + k) % N_Z, me), at((y + k) % N_Y, z, me), at(y, z, (me + k) % N_MP)):
            pl.semaphore_signal(barrier, inc=1, device_id=target, device_id_type=MESH)
    pl.semaphore_wait(barrier, 21)

    def send(src, dst, send_sem, recv_sem, target):
        copy = pltpu.make_async_remote_copy(
            src_ref=src, dst_ref=dst, send_sem=send_sem, recv_sem=recv_sem,
            device_id=target, device_id_type=MESH,
        )
        copy.start()
        pending.append(copy)

    def arrived(dst, send_sem, recv_sem, source):
        pltpu.make_async_remote_copy(
            src_ref=dst, dst_ref=dst, send_sem=send_sem, recv_sem=recv_sem,
            device_id=source, device_id_type=MESH,
        ).wait_recv()

    def first_piece(gather, stream, step, shift):
        bufs = gather[0]
        away = (1 if stream % 2 == 0 else -1) * (step - shift)
        if stream < 2:
            block = bufs[0].at[y, (z + 8 - away) % N_Z]
        else:
            block = bufs[1].at[(y + 8 - away) % N_Y, z]
        if step < 4:
            return block
        half = bufs[0].shape[2] // 2
        return block.at[pl.ds(stream % 2 * half, half)]

    def first_start(gather, step):
        for stream in range(4):
            ref = first_piece(gather, stream, step, 1)
            send(ref, ref, gather[2].at[stream, step], gather[3].at[stream, step], targets[stream])

    def first_own(gather):
        first_start(gather, 1)
        for stream in range(4):
            ref = first_piece(gather, stream, 2, 2)
            send(ref, ref, gather[2].at[stream, 2], gather[3].at[stream, 2], two_away[stream])

    def first_all(gather):
        for k in NEAR:
            for i, target in enumerate((at(y, (z + k) % N_Z, me), at((y + k) % N_Y, z, me))):
                ref = gather[0][i].at[y, z]
                send(ref, ref, gather[2].at[i, k], gather[3].at[i, (z, y)[i]], target)

    def first_all_wait(gather):
        for k in NEAR:
            for i in range(2):
                other = ((z, y)[i] + k) % 8
                where = (y, other) if i == 0 else (other, z)
                arrived(gather[0][i].at[where], gather[2].at[i, 0], gather[3].at[i, other], at(*where, me))

    def first_turn(gather, step):
        for stream in range(4):
            ref = first_piece(gather, stream, step, 0)
            arrived(ref, gather[2].at[stream, step], gather[3].at[stream, step], targets[stream ^ 1])
        if step in (2, 3):
            first_start(gather, step + 1)

    def piece(gather, stream, unit, shift):
        bufs, parts = gather[0], gather[1]
        away = (1 if stream % 2 == 0 else -1) * (unit[0] - shift)
        width = 8 // parts
        mine, across = (z, y) if stream < 2 else (y, z)
        toward = 2 * (mine % 2) - 1
        turn = (0, toward, -toward, 2)[unit[1]]
        span = pl.ds((mine // width + parts + turn) % parts * width, width)
        if stream < 2:
            return bufs[0].at[(across + 8 - away) % N_Y, span]
        return bufs[1].at[span, (across + 8 - away) % N_Z]

    def ring_start(gather, stream, unit):
        index = ring_units(gather[1], 1 if stream % 2 == 0 else -1).index(unit)
        ref = piece(gather, stream, unit, 1)
        send(ref, ref, gather[4].at[stream, index], gather[5].at[stream, index], targets[stream ^ 2])

    def inject(gather, part):
        for stream in range(4):
            ring_start(gather, stream, (1, part))

    def ring_turn(gather, index):
        for stream in range(4):
            units = ring_units(gather[1], 1 if stream % 2 == 0 else -1)
            step, part = units[index]
            ref = piece(gather, stream, (step, part), 0)
            arrived(ref, gather[4].at[stream, index], gather[5].at[stream, index], targets[stream ^ 3])
            if (step + 1, part) in units:
                ring_start(gather, stream, (step + 1, part))

    two_away = (at(y, (z + 2) % N_Z, me), at(y, (z + 6) % N_Z, me), at((y + 2) % N_Y, z, me), at((y + 6) % N_Y, z, me))

    def chunk(gather, stream, step, shift):
        away = (1 if stream % 2 == 0 else -1) * (step - shift)
        span = pl.ds(stream % 2 * 4, 4) if step == 4 else pl.ds(0, 8)
        if stream < 2:
            return gather[0][0].at[(y + 8 - away) % N_Y, span]
        return gather[0][1].at[span, (z + 8 - away) % N_Z]

    def chunk_send(gather, stream, step, shift):
        ref = chunk(gather, stream, step, shift)
        target = (two_away if shift == 2 else targets)[stream ^ 2]
        send(ref, ref, gather[4].at[stream, step], gather[5].at[stream, step], target)

    def chunk_wait(gather, step):
        for stream in range(4):
            ref = chunk(gather, stream, step, 0)
            arrived(ref, gather[4].at[stream, step], gather[5].at[stream, step], targets[stream ^ 3])

    def second_start(gather):
        for step in (1, 2):
            for stream in range(4):
                chunk_send(gather, stream, step, step)

    def second_turn(gather):
        chunk_wait(gather, 2)
        for step in (3, 4):
            for stream in range(4):
                chunk_send(gather, stream, step, step - 2)

    def second_wait(gather):
        for step in (1, 3, 4):
            chunk_wait(gather, step)

    kv = ((kbuf, vbuf), 4, first_send, first_recv, ring_send, ring_recv)
    tile_f = ((tiles.at[0], tiles.at[1]), 1, tile_first_send.at[0], tile_first_recv.at[0], tile_ring_send.at[0], tile_ring_recv.at[0])
    tile_b = ((tiles.at[2], tiles.at[3]), 1, tile_first_send.at[1], tile_first_recv.at[1], tile_ring_send.at[1], tile_ring_recv.at[1])

    def part_send(which, peer, k):
        send(
            part_buf.at[which, pl.ds(pl.multiple_of(peer * ROWS, ROWS), ROWS)],
            part_recv.at[which, me],
            part_send_sem.at[which, k], part_recv_sem.at[which, me], at(y, z, peer),
        )

    def part_sum(which):
        total = part_buf[which, pl.ds(pl.multiple_of(me * ROWS, ROWS), ROWS)].astype(f32)
        for k in ORDER:
            peer = (me + k) % N_MP
            arrived(part_recv.at[which, peer], part_send_sem.at[which, 0], part_recv_sem.at[which, peer], at(y, z, peer))
            total = total + part_recv[which, peer].astype(f32)
        return total

    def stat_start(which, row):
        stat_buf[which] = row
        for k in ORDER:
            peer = (me + k) % N_MP
            send(
                stat_buf.at[which], stat_recv.at[which, me],
                stat_send_sem.at[which, k], stat_recv_sem.at[which, me], at(y, z, peer),
            )

    def stat_sum(which):
        total = stat_buf[which]
        for k in ORDER:
            peer = (me + k) % N_MP
            arrived(stat_recv.at[which, peer], stat_send_sem.at[which, 0], stat_recv_sem.at[which, peer], at(y, z, peer))
            total = total + stat_recv[which, peer]
        return total

    sibling = me + 1 - 2 * (me % 2)

    def rows_send(which, src, k, slot, target):
        send(
            src, rows_recv.at[which, slot], rows_send_sem.at[which, k], rows_recv_sem.at[which, slot], at(y, z, target)
        )

    def rows_start(which, rows):
        rows_recv[which, me] = rows
        for k in (4, 2, 6):
            rows_send(which, rows_recv.at[which, me], k, me, (me + k) % N_MP)
        rows_send(which, rows_recv.at[which, me], 0, me, sibling)

    def rows_wait(which, source):
        arrived(
            rows_recv.at[which, source], rows_send_sem.at[which, 0], rows_recv_sem.at[which, source], at(y, z, source)
        )

    def rows_forward(which):
        for k in (2, 6, 4):
            source = (me + k) % N_MP
            rows_wait(which, source)
            rows_send(which, rows_recv.at[which, source], k + 1, source, sibling)

    def rows_product(which, product, wait=True):
        total = product(rows_recv[which, me], me)
        for k in (2, 6, 4):
            source = (me + k) % N_MP
            total = total + product(rows_recv[which, source], source)
        for k in (0, 2, 6, 4):
            source = (sibling + k) % N_MP
            if wait:
                rows_wait(which, source)
            total = total + product(rows_recv[which, source], source)
        return total

    def drain(until=None):
        for copy in pending[:until]:
            copy.wait_send()
        del pending[:until]

    def project(which, product, peers=ORDER + (0,)):
        for k in peers:
            peer = (me + k) % N_MP
            cols = product(pl.ds(pl.multiple_of(peer * 256, 256), 256)).astype(bf16)
            part_buf[which, pl.ds(pl.multiple_of(peer * ROWS, ROWS), ROWS)] = stack(cols)
            if k:
                part_send(which, peer, k)

    def query_cols(rows):
        return lambda cols: dot(rows, wq_ref[:, cols])

    def grad_cols(rows):
        return lambda cols: dot_t(rows, wo_ref[cols, :])

    live2 = jnp.where(depth_ref[0] >= 2, 1.0, 0.0).astype(f32)
    live3 = jnp.where(depth_ref[0] >= 3, 1.0, 0.0).astype(f32)

    def keys_at(c):
        return kbuf[c].reshape(CHUNK, HD)

    def values_at(c):
        return vbuf[c].reshape(CHUNK, HD)

    shape = (ROWS, CHUNK)

    def scores(query, c):
        s = dot_t(query, keys_at(c))
        sbuf[c] = s
        best_ref[...] = jnp.maximum(best_ref[...], lane_max(s))

    def own_scores(query):
        s = dot_t(query, keys_at(y))
        token = lax.broadcasted_iota(jnp.int32, shape, 0) % TOK + z * TOK
        s = jnp.where(lax.broadcasted_iota(jnp.int32, shape, 1) <= token, s, very_low)
        sbuf[y] = s
        best_ref[...] = lane_max(s)

    def step_scores(query, step):
        @pl.when(y >= step)
        def _():
            scores(query, y - step)

        if step < 4:
            @pl.when(y + step >= N_Y)
            def _():
                scores(query, y + step - N_Y)

    def weigh(level, factor):
        best = jnp.max(best_ref[...], axis=1, keepdims=True)
        if factor is not None:
            best = best * factor

        def weights(c):
            s = sbuf[c]
            if factor is not None:
                s = s * factor
            p = jnp.exp2(s - best)
            total = lane_fold(p)
            p = p.astype(bf16)
            pbuf[level, c] = p
            return total, dot(p, values_at(c))

        def two(i, carry):
            first, second = weights(2 * i), weights(2 * i + 1)
            return carry[0] + first[0] + second[0], carry[1] + first[1] + second[1]

        def one(c, carry):
            first = weights(c)
            return carry[0] + first[0], carry[1] + first[1]

        count = y + 1
        carry = lax.fori_loop(0, count // 2, two, (jnp.zeros((ROWS, 128), f32), jnp.zeros((ROWS, HD), f32)))
        total, accum = lax.fori_loop(count // 2 * 2, count, one, carry)
        share = 1.0 / jnp.sum(total, axis=1, keepdims=True)
        return (accum * share).astype(bf16), share

    def backward(level, grad_att, attended, share):
        delta = jnp.sum(grad_att.astype(f32) * attended.astype(f32), axis=1, keepdims=True)

        def grads(c):
            dprobs = dot_t(grad_att, values_at(c))
            ds = (pbuf[level, c].astype(f32) * (dprobs - delta)).astype(bf16)
            return dot(ds, keys_at(c))

        count = y + 1
        accum = lax.fori_loop(
            0, count // 2, lambda i, a: a + grads(2 * i) + grads(2 * i + 1), jnp.zeros((ROWS, HD), f32)
        )
        accum = lax.fori_loop(count // 2 * 2, count, lambda c, a: a + grads(c), accum)
        return (accum * (share * SCALE)).astype(bf16)

    def head_cols(j):
        return pl.ds(pl.multiple_of(j * ROWS, ROWS), ROWS)

    def out_product(rows, j):
        return dot(rows, wo_ref[head_cols(j), :])

    def query_product(rows, j):
        return dot_t(rows, wq_ref[:, head_cols(j)])

    def tile_product(first):
        def product(rows, j):
            return jnp.concatenate(
                [dot(rows, tiles[first + half, j].reshape(ROWS, HD)) for half in range(2)], axis=0
            )
        return product

    def inverse_of(which):
        return lax.rsqrt(stat_sum(which) * (1.0 / D) + epsilon)

    def twice(a):
        return jnp.concatenate([a, a], axis=0)

    loads[0].wait()
    loads[1].wait()
    first_own(kv)
    for load in loads[2:5]:
        load.wait()
    x_f = x_ref[...].astype(f32)
    gain = gain_ref[...]
    project(0, query_cols((x_f * gain).astype(bf16)))
    stat_start(0, row_stat(x_f * x_f))
    first_turn(kv, 1)
    inject(kv, 0)
    for load in loads[5:]:
        load.wait()
    cot = cot_ref[...]
    project(1, grad_cols(cot), ORDER[:3])
    first_turn(kv, 2)
    inject(kv, 1)
    project(1, grad_cols(cot), ORDER[3:] + (0,))
    first_turn(kv, 3)
    inject(kv, 2)
    rows_f = dot((wo_ref[pl.ds(pl.multiple_of(seq * TILE, TILE), TILE), :].astype(f32) * gain).astype(bf16), wq_ref[...])
    ring_turn(kv, 0)
    first_turn(kv, 4)
    inject(kv, 3)
    group = wq_ref[:, pl.ds(pl.multiple_of(seq // 4 * 128, 128), 128)]
    turned[...] = (group.astype(f32).T * gain).astype(bf16)
    rows_b = dot_t(turned[pl.ds(pl.multiple_of(seq % 4 * TILE, TILE), TILE), :], wo_ref[...])
    ring_turn(kv, 1)
    for h in range(N_MP):
        for i, rows in enumerate((rows_f, rows_b)):
            for half in range(2):
                start = h * ROWS + half * HD
                tile_buf[h, 2 * i + half] = rows[:, start : start + HD].astype(bf16)
    for k in ORDER:
        peer = (me + k) % N_MP
        send(tile_buf.at[peer], tile_recv.at[me], tile_send_sem.at[k], tile_recv_sem.at[me], at(y, z, peer))
    ring_turn(kv, 2)
    raw2 = part_sum(0)
    inverse2 = inverse_of(0)
    query2 = (raw2 * (twice(spread(inverse2)) * (SCALE * LOG2E))).astype(bf16)
    ring_turn(kv, 3)
    own_scores(query2)
    ring_turn(kv, 4)
    step_scores(query2, 1)
    ring_turn(kv, 5)
    tile = tile_buf[me].astype(f32)
    for k in ORDER:
        peer = (me + k) % N_MP
        arrived(tile_recv.at[peer], tile_send_sem.at[0], tile_recv_sem.at[peer], at(y, z, peer))
        tile = tile + tile_recv[peer].astype(f32)
    for i in range(4):
        tiles[i, y, z] = tile[i].astype(bf16)
    first_all(tile_f)
    ring_turn(kv, 6)
    grad_att3 = part_sum(1)
    ring_turn(kv, 7)
    step_scores(query2, 2)
    mark = len(pending)
    ring_turn(kv, 8)
    drain(mark // 2)
    ring_turn(kv, 9)
    ring_turn(kv, 10)
    ring_turn(kv, 11)
    first_all_wait(tile_f)
    mark = len(pending)
    second_start(tile_f)
    step_scores(query2, 3)
    ring_turn(kv, 12)
    drain(mark - 16)
    ring_turn(kv, 13)
    step_scores(query2, 4)

    attended2, share2 = weigh(0, None)
    rows_start(0, side(attended2))
    second_turn(tile_f)
    rows_forward(0)
    x3 = (x_ref[...].astype(f32) + live2 * rows_product(0, out_product)).astype(bf16)
    state3[...] = x3
    x3_f = x3.astype(f32)
    stat_start(1, row_stat(x3_f * x3_f))

    first_all(tile_b)
    project(2, grad_cols(x3))
    second_wait(tile_f)
    raw3 = raw2 + live2 * rows_product(0, tile_product(0), wait=False)
    query3 = (raw3 * (SCALE * LOG2E)).astype(bf16)
    own_scores(query3)

    first_all_wait(tile_b)
    second_start(tile_b)

    def score_two(i, carry):
        first, second = dot_t(query3, keys_at(2 * i)), dot_t(query3, keys_at(2 * i + 1))
        sbuf[2 * i] = first
        sbuf[2 * i + 1] = second
        best_ref[...] = jnp.maximum(best_ref[...], jnp.maximum(lane_max(first), lane_max(second)))
        return carry

    def score_one(c, carry):
        scores(query3, c)
        return carry

    lax.fori_loop(0, y // 2, score_two, 0)
    lax.fori_loop(y // 2 * 2, y, score_one, 0)
    mark = len(pending)
    inverse3 = inverse_of(1)
    factor3 = twice(spread(inverse3))[:, :1]
    attended3, share3 = weigh(1, factor3)
    grad_query3 = backward(1, (grad_att3 * live3).astype(bf16), attended3, share3)
    rows_start(2, side(grad_query3))
    stat_start(2, row_stat(side(grad_query3.astype(f32) * raw3)))
    second_turn(tile_b)
    state_part = part_sum(2)
    drain(mark // 2)
    rows_forward(2)
    drain(mark - mark // 2)
    second_wait(tile_b)

    through = rows_product(2, tile_product(2))
    inner3 = stat_sum(2)
    coef3 = inverse3 * inverse3 * inverse3 * inner3 * (1.0 / D)
    grad_att2 = live2 * (grad_att3 + twice(spread(inverse3)) * through - twice(spread(coef3)) * state_part)
    rows_start(1, side(attended3))
    grad_query2 = backward(0, grad_att2.astype(bf16), attended2, share2)
    mark = len(pending)
    rows_start(3, side(grad_query2))
    stat_start(3, row_stat(side(grad_query2.astype(f32) * raw2)))
    rows_forward(1)
    mixed_ref[...] = (state3[...].astype(f32) + live3 * rows_product(1, out_product)).astype(bf16)

    def grad_input(which, wait, state, inverse, coef, grad_f):
        inv = widen(spread(inverse), PART // 128)
        rest = grad_f - state.astype(f32) * widen(spread(coef), PART // 128)
        return (rest + inv * gain * rows_product(which, query_product, wait)).astype(bf16)

    grad3 = grad_input(2, False, state3[...], inverse3, coef3, cot_ref[...].astype(f32))
    drain(mark)
    rows_forward(3)
    inner2 = stat_sum(3)
    coef2 = inverse2 * inverse2 * inverse2 * inner2 * (1.0 / D)
    grad_ref[...] = grad_input(3, True, x_ref[...], inverse2, coef2, grad3.astype(f32))
    drain()


def shards(hidden, keys, values, norm_gain, w_query, w_out, depth, cotangent):
    any_spec = pl.BlockSpec(memory_space=pl.ANY)
    vmem_spec = pl.BlockSpec(memory_space=pltpu.VMEM)
    sem = pltpu.SemaphoreType.DMA
    out = jax.ShapeDtypeStruct((TOK, PART), bf16)
    mixed, grad = pl.pallas_call(
        kernel,
        out_shape=(out, out),
        in_specs=[any_spec] * 6 + [pl.BlockSpec(memory_space=pltpu.SMEM), any_spec],
        out_specs=(vmem_spec, vmem_spec),
        scratch_shapes=[
            pltpu.VMEM((TOK, PART), bf16),
            pltpu.VMEM((1, PART), f32),
            pltpu.VMEM((PART, HEADS), bf16),
            pltpu.VMEM((HEADS, PART), bf16),
            pltpu.VMEM((TOK, PART), bf16),
            pltpu.VMEM((N_Y, N_Z, TOK, HD), bf16),
            pltpu.VMEM((N_Y, N_Z, TOK, HD), bf16),
            pltpu.VMEM((N_Y, ROWS, CHUNK), f32),
            pltpu.VMEM((2, N_Y, ROWS, CHUNK), bf16),
            pltpu.VMEM((ROWS, 128), f32),
            pltpu.VMEM((3, HEADS, HD), bf16),
            pltpu.VMEM((3, N_MP, ROWS, HD), bf16),
            pltpu.VMEM((4, 8, TOK), f32),
            pltpu.VMEM((4, N_MP, 8, TOK), f32),
            pltpu.VMEM((4, N_MP, TOK, ROWS), bf16),
            pltpu.VMEM((128, PART), bf16),
            pltpu.VMEM((N_MP, 4, TILE, HD), bf16),
            pltpu.VMEM((N_MP, 4, TILE, HD), bf16),
            pltpu.VMEM((4, N_Y, N_Z, TILE, HD), bf16),
            pltpu.VMEM((TOK, PART), bf16),
            sem((7,)),
            sem((4, 5)), sem((4, 5)), sem((2, 2, 8)), sem((2, 2, 8)),
            sem((4, 14)), sem((4, 14)), sem((2, 4, 5)), sem((2, 4, 5)),
            sem((3, 8)), sem((3, 8)), sem((4, 8)), sem((4, 8)), sem((4, 8)), sem((4, 8)),
            sem((8,)), sem((8,)),
        ],
        compiler_params=pltpu.CompilerParams(
            collective_id=0, has_side_effects=True, vmem_limit_bytes=60 * 1024 * 1024
        ),
        name="recursion",
    )(hidden, keys, values, norm_gain.reshape(1, PART), w_query, w_out, depth, cotangent)
    live = depth[0] >= 2
    return jnp.where(live, mixed, hidden), jnp.where(live, grad, cotangent)


def solution(mesh):
    return jax.shard_map(
        shards,
        mesh=mesh,
        in_specs=(
            P("seq", "mp"),
            P("seq", "mp"),
            P("seq", "mp"),
            P("mp"),
            P("mp", None),
            P(None, "mp"),
            P("seq"),
            P("seq", "mp"),
        ),
        out_specs=(P("seq", "mp"), P("seq", "mp")),
        check_vma=False,
    )
```
